256 devices in a mesh: section: 8 (over y, core), seq: 32 (over x, z).
Axes of the slice: x: 4, y: 4, z: 8, core: 2. Of those that a mesh axis runs over, the one named last changes fastest.
Arguments:
- queries: bfloat16 [8, 4096, 2048], P('section', 'seq'), may hold values from -4 to 4
- memory_keys: bfloat16 [8, 4096, 2048], P('section', 'seq'), may hold values from -2.5 to 2.5
- memory_values: bfloat16 [8, 4096, 2048], P('section', 'seq'), may hold values from -4 to 4
- upstream: bfloat16 [8, 4096, 2048], P('section', 'seq'), may hold values from -4 to 4
- inner_rate: float32 [8, 32], P('section'), may hold values from 0.02 to 0.2
- checkpoints: float32 [8, 32, 32, 4096], P('section', 'seq'), may hold values from -0.75 to 0.75
Outputs:
- grad_queries: bfloat16 [8, 4096, 2048], P('section', 'seq')
- grad_keys: bfloat16 [8, 4096, 2048], P('section', 'seq')
- grad_values: bfloat16 [8, 4096, 2048], P('section', 'seq')
- adjoint_start: float32 [8, 32, 32, 4096], P('section', 'seq')
The draws below stay inside these ranges and needn't reach their ends.
All inputs are finite; a program needn't handle non-finite values.
Results may differ from the reference program's by a relative error of at most 0.001.
Values may be sent and summed in bfloat16 or wider, within the bound.
No kernel may reach another device: no remote copies, remote signals or barrier semaphores. Data moves between devices by JAX's collectives and lax.ppermute only.
A program may use at most 128 MiB of HBM per device.

```python
import math
from functools import partial
import jax
import jax.numpy as jnp
from jax import lax

H = 32
DH = 64
MB = 64
TOK_DEV = 128
SECTIONS = 8
SHARDS = 32
TOKENS = 4096
HD = 2048


def shard_levels(own_key, shape, shards, low, high):
    level = 1.0
    for position, shards_of in shards:
        draws = jax.random.uniform(jax.random.fold_in(jax.random.fold_in(own_key, 6), position), (shards_of,), jnp.float32, low / len(shards), high / len(shards))
        level = level * jnp.repeat(jnp.exp(draws), shape[position] // shards_of).reshape((-1,) + (1,) * (len(shape) - 1 - position))
    return level


def centred(key, dims, deviation, limit, cuts=(), kind=jnp.bfloat16):
    loudness = shard_levels(key, dims, cuts, -0.22, 0.18) if cuts else 1.0
    values = jax.random.normal(key, dims, jnp.float32) * deviation * loudness
    return jnp.minimum(jnp.maximum(values, -limit), limit).astype(kind)


def setup_inputs(seed: int = 0) -> dict:
    key_list = jax.random.split(jax.random.key(seed), 7)
    queries = centred(key_list[0], (SECTIONS, TOKENS, HD), 1.0, 4.0, ((0, 8), (1, 32)))
    memory_keys = centred(key_list[1], (SECTIONS, TOKENS, HD), 1.0, 2.5, ((0, 8), (1, 32)))
    memory_values = centred(key_list[2], (SECTIONS, TOKENS, HD), 1.0, 4.0, ((0, 8), (1, 32)))
    upstream = centred(key_list[3], (SECTIONS, TOKENS, HD), 1.0, 4.0, ((0, 8), (1, 32)))
    inner_rate = jnp.clip(jnp.exp(math.log(0.2) - 2.3025851 * jax.random.uniform(key_list[4], (SECTIONS, H), jnp.float32) ** shard_levels(key_list[4], (SECTIONS, H), ((0, 8),), -0.2, 0.2)), 0.02, 0.2)
    checkpoints = centred(key_list[5], (SECTIONS, SHARDS, H, DH * DH), DH ** -0.5, 0.75, ((0, 8), (1, 32)), jnp.float32)
    return {"queries": queries, "memory_keys": memory_keys, "memory_values": memory_values, "upstream": upstream, "inner_rate": inner_rate, "checkpoints": checkpoints}


inner_product = partial(jnp.einsum, precision=lax.Precision.HIGHEST)


def lower_mask():
    row_index = lax.broadcasted_iota(jnp.int32, (MB, MB), 0)
    col_index = lax.broadcasted_iota(jnp.int32, (MB, MB), 1)
    return (row_index >= col_index).astype(jnp.float32)


def to_blocks(array):
    shaped = array.astype(jnp.float32).reshape(TOKENS // MB, MB, H, DH)
    return jnp.transpose(shaped, (0, 2, 1, 3))


def from_blocks(array):
    return jnp.transpose(array, (0, 2, 1, 3)).reshape(TOKENS, H * DH).astype(jnp.bfloat16)


def shard_major(array):
    per_shard = TOK_DEV // MB
    shaped = array.reshape((SHARDS, per_shard) + array.shape[1:])
    return jnp.swapaxes(shaped, 0, 1)


def block_major(array):
    return jnp.swapaxes(array, 0, 1).reshape((TOKENS // MB,) + array.shape[2:])


def one_section(operands):
    queries, memory_keys, memory_values, cotangent, inner_rate, checkpoints = operands
    per_shard = TOK_DEV // MB
    update_rate = (inner_rate / MB)[:, None, None]
    masked_scores = lower_mask()
    query_blocks = to_blocks(queries)
    key_blocks = to_blocks(memory_keys)
    value_blocks = to_blocks(memory_values)
    grad_blocks = to_blocks(cotangent)
    initial = checkpoints.reshape(SHARDS, H, DH, DH)

    def forward(weight_stack, pieces):
        current_key, current_value = pieces
        error_rows = inner_product("shmd,shde->shme", current_key, weight_stack) - current_value
        updated_weight = weight_stack - update_rate * inner_product("shmd,shme->shde", current_key, error_rows)
        return updated_weight, (weight_stack, error_rows)

    trails = lax.scan(forward, initial, (shard_major(key_blocks), shard_major(value_blocks)))[1]
    weight_trail = block_major(trails[0])
    error_trail = block_major(trails[1])

    def backward(adjoint_carry, pieces):
        current_query, current_key, current_gradient, current_weight, error_now = pieces
        attention_scores = inner_product("sxi,sbi->sxb", current_query, current_key) * masked_scores
        error_gradient = -update_rate * (inner_product("hmn,hme->hne", attention_scores, current_gradient) + inner_product("hnd,hde->hne", current_key, adjoint_carry))
        score_gradient = -update_rate * inner_product("hme,hne->hmn", current_gradient, error_now) * masked_scores
        query_gradient = inner_product("nyv,nxv->nyx", current_gradient, current_weight) + inner_product("clo,coq->clq", score_gradient, current_key)
        grad_key = (inner_product("hne,hde->hnd", error_gradient, current_weight)
                    - update_rate * inner_product("hne,hde->hnd", error_now, adjoint_carry)
                    + inner_product("fbw,fbe->fwe", score_gradient, current_query))
        previous_weight = adjoint_carry + inner_product("fwl,fwn->fln", current_query, current_gradient) + inner_product("wik,wiy->wky", current_key, error_gradient)
        return previous_weight, (query_gradient, grad_key, -error_gradient, previous_weight)

    empty = jnp.zeros((H, DH, DH), jnp.float32)
    results = lax.scan(backward, empty, (query_blocks, key_blocks, grad_blocks, weight_trail, error_trail), reverse=True)[1]
    starts = results[3].reshape(SHARDS, per_shard, H, DH, DH)[:, 0].reshape(SHARDS, H, DH * DH)
    return from_blocks(results[0]), from_blocks(results[1]), from_blocks(results[2]), starts


def reference(queries, memory_keys, memory_values, upstream, inner_rate, checkpoints):
    cotangent = jnp.roll(upstream, -1, axis=0)
    grad_queries, grad_keys, grad_values, adjoint_start = lax.map(
        one_section, (queries, memory_keys, memory_values, cotangent, inner_rate, checkpoints))
    return grad_queries, grad_keys, grad_values, adjoint_start
```

```python
from functools import partial

import jax
import jax.numpy as jnp
from jax import lax
from jax.experimental import pallas as pl
from jax.experimental.pallas import tpu as pltpu
from jax.sharding import PartitionSpec as P

DH = 64
QUAD = 4 * DH
PAIRS = QUAD // 128
HEADS = QUAD // DH
F32 = jnp.float32
BF16 = jnp.bfloat16
CHUNKS = 4
CODE_SPAN = 250.0
CODE_BASE = -125.0


def quad_iota():
    row = lax.broadcasted_iota(jnp.int32, (DH, QUAD), 0)
    lane = lax.broadcasted_iota(jnp.int32, (DH, QUAD), 1)
    return row, lane % DH, lane // DH


def head_masks():
    head = quad_iota()[2]
    return [(head == h).astype(F32).astype(BF16) for h in range(QUAD // DH)]


def diagonal(right, masks):
    return jnp.concatenate([right * mask for mask in masks], axis=0)


def times(left, block):
    return lax.dot_general(left, block, (((1,), (0,)), ((), ())), preferred_element_type=F32)


def times_t(left, block):
    return lax.dot_general(left, block, (((1,), (1,)), ((), ())), preferred_element_type=F32)


def split(value):
    high = value.astype(BF16)
    low = (value - high.astype(F32)).astype(BF16)
    return high, low


def both(high, low):
    return jnp.concatenate([high, low], axis=0)


def folded(product):
    return product[:DH] + product[DH:]


def column_scale(value):
    largest = jnp.max(jnp.abs(value), axis=0, keepdims=True)
    return (jnp.maximum(largest, 1e-30) * 1.01).astype(BF16).astype(F32)


def encode(value, scale):
    size = jnp.exp2(jnp.abs(value) * (CODE_SPAN / scale) + CODE_BASE)
    return jnp.where(value < 0, -size, size)


def decode(code, scale):
    size = (jnp.log2(jnp.abs(code)) - CODE_BASE) * (scale / CODE_SPAN)
    return jnp.where(code < 0, -size, size)


def chunk(ref, i, features):
    if ref.shape[1] != features:
        size = ref.shape[0] // CHUNKS
        return ref.at[pl.ds(pl.multiple_of(i * size, size), size), :]
    size = features // CHUNKS
    return ref.at[:, pl.ds(pl.multiple_of(i * size, size), size)]


def rates(rate_ref, index):
    head = lax.broadcasted_iota(jnp.int32, (DH, QUAD), 1) // DH
    value = jnp.full((DH, QUAD), rate_ref[0, index * HEADS], F32)
    for h in range(1, HEADS):
        value = jnp.where(head == h, rate_ref[0, index * HEADS + h], value)
    return value * (1.0 / DH)


def mover(sources, targets, sems, features):
    def copies(i):
        return [
            pltpu.make_async_copy(chunk(source, i, features), chunk(target, i, features), sems.at[n, i])
            for n, (source, target) in enumerate(zip(sources, targets))
        ]

    def start(i):
        for copy in copies(i):
            copy.start()

    def wait(i):
        for copy in copies(i):
            copy.wait()

    return start, wait


def run(work, count, fetch=None, ship=None):
    each = count // CHUNKS
    if fetch is not None:
        fetch[0](0)
        fetch[0](1)

    def body(i, carry):
        if fetch is not None:
            fetch[1](i)

            @pl.when(i + 2 < CHUNKS)
            def _():
                fetch[0](i + 2)

        for t in range(each):
            index = i * each + t
            work(index, pl.ds(pl.multiple_of(index * QUAD, QUAD), QUAD), t)
        if ship is not None:
            ship[0](i)
        return carry

    lax.fori_loop(0, CHUNKS, body, 0)
    if ship is not None:
        for i in range(CHUNKS):
            ship[1](i)


def map_kernel(q_hbm, k_hbm, rate_ref, acode_ref, ascale_ref, mt_ref, q_ref, k_ref, in_sems):
    row, col, _ = quad_iota()
    masks = head_masks()
    identity = (row == col).astype(F32).astype(BF16)
    upper = (row <= col).astype(F32)

    def work(index, lanes, t):
        rate = rates(rate_ref, index)
        gates, readouts = [], []
        for b in range(2):
            rows = slice(b * DH, (b + 1) * DH)
            k, q = k_ref[rows, lanes], q_ref[rows, lanes]
            k_block, q_block = diagonal(k, masks), diagonal(q, masks)
            on_q = times_t(both(k, identity), q_block)
            st_hi, st_lo = split(on_q[:DH] * upper)
            qt = on_q[DH:]
            kt = times_t(identity, k_block).astype(BF16)
            gates.append(rate * times(kt, k_block))
            readouts.append(qt - rate * (times(kt, diagonal(st_hi, masks)) + times(kt, diagonal(st_lo, masks))))
        g_hi, g_lo = split(gates[0])
        g_both = both(g_hi, g_lo)

        def gate_times(value):
            hi, lo = split(value)
            return folded(times(g_both, diagonal(hi, masks))) + times(g_hi, diagonal(lo, masks))

        drop = gates[0] + gates[1] - gate_times(gates[1])
        second = readouts[1] - gate_times(readouts[1])
        for b, value in enumerate((readouts[0], second)):
            hi, lo = split(value)
            mt_ref[b * 128 : b * 128 + 64, lanes] = hi
            mt_ref[b * 128 + 64 : b * 128 + 128, lanes] = lo
        scale = column_scale(drop)
        acode_ref[:, lanes] = encode(drop, scale).astype(BF16)
        ascale_ref[:, lanes] = jnp.broadcast_to(scale, (8, QUAD))

    features = k_ref.shape[1]
    run(work, features // QUAD, mover((q_hbm, k_hbm), (q_ref, k_ref), in_sems, features))


def pack_kernel(mt_ref, dz_ref, acode_ref, ascale_ref, out_ref):
    masks = head_masks()
    left = lax.broadcasted_iota(jnp.int32, (DH, 128), 1) < DH
    left8 = left[:8]

    def work(index, lanes, t):
        total = folded(times(mt_ref[0:128, lanes], diagonal(dz_ref[0:DH, lanes], masks)))
        total += folded(times(mt_ref[128:256, lanes], diagonal(dz_ref[DH:128, lanes], masks)))
        scale = column_scale(total)
        code = encode(total, scale)
        a_code = acode_ref[:, lanes].astype(F32)
        a_scale = ascale_ref[:, lanes]
        scale = jnp.broadcast_to(scale, (8, QUAD))
        for p in range(PAIRS):
            cut = slice(p * 128, p * 128 + 128)
            head = index * HEADS + p * 2
            out_ref[head, 0:DH, :] = jnp.where(left, a_code[:, cut], pltpu.roll(code[:, cut], DH, 1)).astype(BF16)
            out_ref[head, DH : DH + 8, :] = jnp.where(left8, a_scale[:, cut], pltpu.roll(scale[:, cut], DH, 1)).astype(BF16)
            out_ref[head + 1, 0:DH, :] = jnp.where(left, pltpu.roll(a_code[:, cut], DH, 1), code[:, cut]).astype(BF16)
            out_ref[head + 1, DH : DH + 8, :] = jnp.where(left8, pltpu.roll(a_scale[:, cut], DH, 1), scale[:, cut]).astype(BF16)

    run(work, dz_ref.shape[1] // QUAD)


def relay_kernel(in_ref, out_ref, map_ref, left_ref, group):
    shards = in_ref.shape[0]
    row = lax.broadcasted_iota(jnp.int32, (DH, 128), 0)
    lane = lax.broadcasted_iota(jnp.int32, (DH, 128), 1)
    left = lane < DH
    unit = (row == lane).astype(F32)

    def unpack(j, carry):
        scale = in_ref[j, DH : DH + 8, :].astype(F32)[0:1]
        value = decode(in_ref[j, 0:DH, :].astype(F32), scale)
        value = jnp.where(left, unit - value, value)
        map_ref[j] = value
        left_ref[j] = left_operand(value)
        return carry

    def left_operand(value):
        hi, lo = split(value)
        hi_f = hi.astype(F32)
        lo_f = lo.astype(F32)
        first = jnp.where(left, hi_f, pltpu.roll(lo_f, DH, 1)).astype(BF16)
        last = jnp.where(left, hi_f, 0.0).astype(BF16)
        return jnp.concatenate([first, last], axis=1)

    def right_operand(value):
        hi, lo = split(value)
        return jnp.concatenate([hi, hi, lo, jnp.zeros_like(lo)], axis=0)

    lax.fori_loop(0, shards, unpack, 0, unroll=4)
    groups = shards // group
    suffix = [map_ref[g * group + group - 1] for g in range(groups)]
    for step in range(group - 2, -1, -1):
        for g in range(groups):
            j = g * group + step
            own = map_ref[j]
            suffix[g] = times(left_ref[j], right_operand(suffix[g])) + jnp.where(left, 0.0, own)
            map_ref[j] = suffix[g]
            left_ref[j] = left_operand(suffix[g])
    ends = [None] * groups
    ends[groups - 1] = jnp.zeros((DH, 128), F32)
    for g in range(groups - 2, -1, -1):
        j = (g + 1) * group
        ends[g] = times(left_ref[j], right_operand(ends[g + 1])) + map_ref[j]
    for g in range(groups):
        right = right_operand(ends[g])
        found = []
        for step in range(group):
            j = g * group + step
            if step == group - 1:
                found.append(ends[g])
            else:
                found.append(times(left_ref[j + 1], right) + map_ref[j + 1])
        for step in range(0, group, 2):
            pair = jnp.where(left, pltpu.roll(found[step], DH, 1), found[step + 1])
            scale = column_scale(pair)
            code = encode(pair, scale)
            turned = pltpu.roll(code, DH, 1)
            scale = jnp.broadcast_to(scale, (8, 128))
            j = g * group + step
            half = DH // 2
            low = left[:half]
            out_ref[j, 0:half, :] = jnp.where(low, code[:half], turned[half:]).astype(BF16)
            other = pltpu.roll(scale, DH, 1)
            out_ref[j, half : half + 8, :] = jnp.where(left[:8], scale, other).astype(BF16)
            out_ref[j + 1, 0:half, :] = jnp.where(low, turned[:half], code[half:]).astype(BF16)
            out_ref[j + 1, half : half + 8, :] = jnp.where(left[:8], other, scale).astype(BF16)


def trail_kernel(rate_ref, *refs):
    inputs, outputs, (flat_ref, in_sems, out_sems) = refs[:5], refs[5:10], refs[20:]
    q_ref, k_ref, v_ref, w_ref, dz_ref = refs[10:15]
    e_ref, wt_ref, kt_ref, t_ref, outer_ref = refs[15:20]
    row, col, _ = quad_iota()
    masks = head_masks()
    identity = (row == col).astype(F32).astype(BF16)
    upper = (row <= col).astype(F32)
    half = DH // 2
    low = lax.broadcasted_iota(jnp.int32, (half, 128), 1) < DH

    def start_weight(pair):
        first = pl.multiple_of(pair * DH, DH)
        one = flat_ref[pl.ds(first, half), :]
        two = flat_ref[pl.ds(first + half, half), :]
        even = jnp.where(low, one, pltpu.roll(two, DH, 1))
        odd = jnp.where(low, pltpu.roll(one, DH, 1), two)
        flat_ref[pl.ds(first, half, stride=2), :] = even
        flat_ref[pl.ds(first + 1, half, stride=2), :] = odd
        return flat_ref[pl.ds(first, DH), :]

    def work(index, lanes, t):
        rate = rates(rate_ref, index)
        if t == 0:
            first = pl.multiple_of(index * HEADS, 8)
            for i in range(half):
                flat_ref[pl.ds(first * half + i, 8, stride=half), :] = w_ref[pl.ds(first, 8), i * 128 : (i + 1) * 128]
        weight = jnp.concatenate([start_weight(index * PAIRS + p) for p in range(PAIRS)], axis=1)
        for b in range(2):
            rows = slice(b * DH, (b + 1) * DH)
            hi_rows, lo_rows = slice(b * 128, b * 128 + 64), slice(b * 128 + 64, b * 128 + 128)
            k = k_ref[rows, lanes]
            w_hi, w_lo = split(weight)
            wt_ref[hi_rows, lanes] = w_hi
            wt_ref[lo_rows, lanes] = w_lo
            error = times(k, diagonal(w_hi, masks)) + times(k, diagonal(w_lo, masks)) - v_ref[rows, lanes].astype(F32)
            e_hi, e_lo = split(error)
            e_ref[hi_rows, lanes] = e_hi
            e_ref[lo_rows, lanes] = e_lo
            kt = times_t(identity, diagonal(k, masks)).astype(BF16)
            kt_ref[rows, lanes] = kt
            if b == 0:
                weight = weight - rate * (times(kt, diagonal(e_hi, masks)) + times(kt, diagonal(e_lo, masks)))
            on_q = times_t(both(k, identity), diagonal(q_ref[rows, lanes], masks))
            st_hi, st_lo = split(on_q[:DH] * upper)
            qt = on_q[DH:].astype(BF16)
            on_dz = times(jnp.concatenate([st_hi, st_lo, qt], axis=0), diagonal(dz_ref[rows, lanes], masks))
            t_ref[rows, lanes] = on_dz[:DH] + on_dz[DH:128]
            outer_ref[rows, lanes] = on_dz[128:]

    features = k_ref.shape[1]
    fetch = mover(inputs, refs[10:15], in_sems, features)
    ship = mover(refs[15:20], outputs, out_sems, features)
    run(work, features // QUAD, fetch, ship)


def direct_kernel(rate_ref, *refs):
    inputs, outputs, (in_sems, out_sems) = refs[:5], refs[5:7], refs[14:]
    q_ref, k_ref, dz_ref, e_ref, wt_ref = refs[7:12]
    gq_ref, part_ref = refs[12:14]
    row, col, _ = quad_iota()
    masks = head_masks()
    upper = (row <= col).astype(F32)
    lower = (row >= col).astype(F32)

    def work(index, lanes, t):
        rate = rates(rate_ref, index)
        for b in range(2):
            rows = slice(b * DH, (b + 1) * DH)
            two = slice(b * 128, b * 128 + 128)
            hi_rows, lo_rows = slice(b * 128, b * 128 + 64), slice(b * 128 + 64, b * 128 + 128)
            dz = dz_ref[rows, lanes]
            dpt = folded(times_t(e_ref[two, lanes], diagonal(dz, masks))) * (-rate * upper)
            dp = times_t(dz, diagonal(e_ref[hi_rows, lanes], masks)) + times_t(dz, diagonal(e_ref[lo_rows, lanes], masks))
            dp = dp * (-rate * lower)
            grad = times_t(dz, diagonal(wt_ref[hi_rows, lanes], masks)) + times_t(dz, diagonal(wt_ref[lo_rows, lanes], masks))
            grad += folded(times(both(*split(dp)), diagonal(k_ref[rows, lanes], masks)))
            gq_ref[rows, lanes] = grad.astype(BF16)
            part_ref[rows, lanes] = folded(times(both(*split(dpt)), diagonal(q_ref[rows, lanes], masks)))

    features = k_ref.shape[1]
    run(work, features // QUAD, mover(inputs, refs[7:12], in_sems, features), mover(refs[12:14], outputs, out_sems, features))


def final_kernel(rate_ref, code_hbm, *refs):
    inputs, outputs = refs[:7], refs[7:10]
    k_ref, kt_ref, e_ref, wt_ref, t_ref, outer_ref, part_ref = refs[10:17]
    gk_ref, gv_ref, start_ref, code_ref, flat_ref, in_sems, out_sems, code_sems = refs[17:]

    def code_copy(i):
        size = code_ref.shape[0] // CHUNKS
        part = pl.ds(i * size, size)
        return pltpu.make_async_copy(code_hbm.at[part], code_ref.at[part], code_sems.at[i])

    masks = head_masks()
    half = DH // 2
    low = lax.broadcasted_iota(jnp.int32, (half, 128), 1) < DH

    def work(index, lanes, t):
        rate = rates(rate_ref, index)
        pairs = []
        for p in range(PAIRS):
            halves = []
            for h in range(2):
                head = index * HEADS + p * 2 + h
                scale = code_ref[head, half : half + 8, :].astype(F32)[0:1]
                halves.append(decode(code_ref[head, 0:half, :].astype(F32), scale))
            top = jnp.where(low, halves[0], pltpu.roll(halves[1], DH, 1))
            bottom = jnp.where(low, pltpu.roll(halves[0], DH, 1), halves[1])
            pairs.append(jnp.concatenate([top, bottom], axis=0))
        adjoint = jnp.concatenate(pairs, axis=1)
        for b in (1, 0):
            rows = slice(b * DH, (b + 1) * DH)
            two = slice(b * 128, b * 128 + 128)
            hi_rows, lo_rows = slice(b * 128, b * 128 + 64), slice(b * 128 + 64, b * 128 + 128)
            g_hi, g_lo = split(adjoint)
            g_block, g_low_block = diagonal(g_hi, masks), diagonal(g_lo, masks)
            k = k_ref[rows, lanes]
            slope = t_ref[rows, lanes] + times(k, g_block) + times(k, g_low_block)
            grad_error = -rate * slope
            gv_ref[rows, lanes] = (-grad_error).astype(BF16)
            d_hi, d_lo = split(grad_error)
            kt = kt_ref[rows, lanes]
            grad = part_ref[rows, lanes]
            grad += folded(times_t(both(d_hi, d_lo), diagonal(wt_ref[hi_rows, lanes], masks)))
            grad += times_t(d_hi, diagonal(wt_ref[lo_rows, lanes], masks))
            on_g = folded(times_t(e_ref[two, lanes], g_block)) + times_t(e_ref[hi_rows, lanes], g_low_block)
            gk_ref[rows, lanes] = (grad - rate * on_g).astype(BF16)
            adjoint = adjoint + outer_ref[rows, lanes] + times(kt, diagonal(d_hi, masks)) + times(kt, diagonal(d_lo, masks))
        for p in range(PAIRS):
            first = pl.multiple_of((index * PAIRS + p) * DH, DH)
            flat_ref[pl.ds(first, DH), :] = adjoint[:, p * 128 : p * 128 + 128]
            even = flat_ref[pl.ds(first, half, stride=2), :]
            odd = flat_ref[pl.ds(first + 1, half, stride=2), :]
            flat_ref[pl.ds(first, half), :] = jnp.where(low, even, pltpu.roll(odd, DH, 1))
            flat_ref[pl.ds(first + half, half), :] = jnp.where(low, pltpu.roll(even, DH, 1), odd)
        if (t + 1) * HEADS == 8:
            head = pl.multiple_of((index + 1) * HEADS - 8, 8)
            for i in range(half):
                start_ref[pl.ds(head, 8), i * 128 : (i + 1) * 128] = flat_ref[pl.ds(head * half + i, 8, stride=half), :]

    features = k_ref.shape[1]
    start, wait = mover(inputs, refs[10:17], in_sems, features)

    def start_all(i):
        code_copy(i).start()
        start(i)

    def wait_all(i):
        code_copy(i).wait()
        wait(i)

    run(work, features // QUAD, (start_all, wait_all), mover((gk_ref, gv_ref, start_ref), outputs, out_sems, features))


def call(kernel, ins, outs, flops, scratch=(), limit=58):
    args = [array for array, _ in ins]
    size = sum(a.size * a.dtype.itemsize for a in args) + sum(o.size * o.dtype.itemsize for o, _ in outs)
    return pl.pallas_call(
        kernel,
        out_shape=tuple(shape for shape, _ in outs),
        in_specs=[pl.BlockSpec(memory_space=memory) for _, memory in ins],
        out_specs=tuple(pl.BlockSpec(memory_space=memory) for _, memory in outs),
        scratch_shapes=list(scratch),
        compiler_params=pltpu.CompilerParams(vmem_limit_bytes=limit * 1024 * 1024),
        cost_estimate=pl.CostEstimate(flops=flops, bytes_accessed=size, transcendentals=0),
    )(*args)


def per_device(queries, memory_keys, memory_values, upstream, inner_rate, checkpoints):
    sections = lax.axis_size("section")
    shards = lax.axis_size("seq")
    heads = inner_rate.shape[1]
    features = queries.shape[2]
    tokens = queries.shape[1]
    q, k, v, w = queries[0], memory_keys[0], memory_values[0], checkpoints[0, 0]

    def array(rows, kind, columns=features):
        return jax.ShapeDtypeStruct((rows, columns), kind)

    def apart(a):
        return jax.ShapeDtypeStruct((a.shape[0] * CHUNKS, a.shape[1] // CHUNKS), a.dtype)

    def buffers(arrays):
        return [pltpu.VMEM(a.shape, a.dtype) for a in arrays]

    def semaphores(count):
        return pltpu.SemaphoreType.DMA((count, CHUNKS))

    def outside(arrays):
        return [(a, pltpu.HBM) for a in arrays]

    def inside(arrays):
        return [(a, pltpu.VMEM) for a in arrays]

    rate = [(inner_rate, pltpu.SMEM)]
    unit = 2 * tokens * features * QUAD
    flat = pltpu.VMEM((heads * DH // 2, 128), F32)
    single, whole, double = array(tokens, F32), array(tokens, BF16), array(2 * tokens, BF16)

    cotangent = lax.ppermute(upstream, "section", [((i + 1) % sections, i) for i in range(sections)])
    dz = cotangent[0]
    acode, ascale, mt = call(
        map_kernel,
        outside([q, k]) + rate,
        inside([array(DH, BF16), array(8, F32), double]),
        8 * unit,
        buffers([q, k]) + [semaphores(2)],
        24,
    )
    (packed,) = call(
        pack_kernel, inside([mt, dz, acode, ascale]), inside([jax.ShapeDtypeStruct((heads, DH + 8, 128), BF16)]), 2 * unit, (), 24
    )
    arrived = lax.all_to_all(packed, "seq", 0, 0, tiled=True)
    rate_later, _ = lax.optimization_barrier((inner_rate, packed))
    given, made = [q, k, v, w, dz], [double, double, whole, single, single]
    error, weights, kt, slope, outer = call(
        trail_kernel,
        [(rate_later, pltpu.SMEM)] + outside(given),
        outside([apart(a) for a in made]),
        10 * unit,
        buffers(given + made) + [flat, semaphores(5), semaphores(5)],
    )
    arrived, slope = lax.optimization_barrier((arrived, slope))
    (ends,) = call(
        partial(relay_kernel, group=8),
        inside([arrived]),
        inside([jax.ShapeDtypeStruct((shards, DH // 2 + 8, 128), BF16)]),
        unit,
        [pltpu.VMEM((shards, DH, 128), F32), pltpu.VMEM((shards, DH, 256), BF16)],
        24,
    )
    returned = lax.all_to_all(ends, "seq", 0, 0, tiled=True)
    rate_later, _ = lax.optimization_barrier((inner_rate, ends))
    given, held, made = [q, k, dz, error, weights], [whole, whole, whole, double, double], [whole, single]
    grad_q, part = call(
        direct_kernel,
        [(rate_later, pltpu.SMEM)] + outside(given),
        outside([whole, apart(single)]),
        10 * unit,
        buffers(held + made) + [semaphores(5), semaphores(2)],
    )
    given, held = [k, kt, error, weights, slope, outer, part], [whole, whole, double, double, single, single, single]
    made = [whole, whole, array(heads, F32, DH * DH)]
    grad_k, grad_v, start = call(
        final_kernel,
        rate + outside([returned] + given),
        outside(made),
        10 * unit,
        buffers(held + made + [returned]) + [flat, semaphores(7), semaphores(3), pltpu.SemaphoreType.DMA((CHUNKS,))],
    )
    return grad_q[None], grad_k[None], grad_v[None], start[None, None]


def solution(mesh):
    tokens = P("section", "seq", None)
    return jax.shard_map(
        per_device,
        mesh=mesh,
        in_specs=(tokens, tokens, tokens, tokens, P("section", None), P("section", "seq", None, None)),
        out_specs=(tokens, tokens, tokens, P("section", "seq", None, None)),
        check_vma=False,
    )
```

```python
from functools import partial

import jax
import jax.numpy as jnp
from jax import lax
from jax.experimental import pallas as pl
from jax.experimental.pallas import tpu as pltpu
from jax.sharding import PartitionSpec as P

DH = 64
QUAD = 4 * DH
PAIRS = QUAD // 128
HEADS = QUAD // DH
F32 = jnp.float32
BF16 = jnp.bfloat16
CHUNKS = 4
MAP_LIMIT = 24
LATE_LIMIT = 24
CODE_SPAN = 250.0
CODE_BASE = -125.0


def quad_iota():
    row = lax.broadcasted_iota(jnp.int32, (DH, QUAD), 0)
    lane = lax.broadcasted_iota(jnp.int32, (DH, QUAD), 1)
    return row, lane % DH, lane // DH


def head_masks():
    head = quad_iota()[2]
    return [(head == h).astype(F32).astype(BF16) for h in range(QUAD // DH)]


def diagonal(right, masks):
    return jnp.concatenate([right * mask for mask in masks], axis=0)


def times(left, block):
    return lax.dot_general(left, block, (((1,), (0,)), ((), ())), preferred_element_type=F32)


def times_t(left, block):
    return lax.dot_general(left, block, (((1,), (1,)), ((), ())), preferred_element_type=F32)


def split(value):
    high = value.astype(BF16)
    low = (value - high.astype(F32)).astype(BF16)
    return high, low


def both(high, low):
    return jnp.concatenate([high, low], axis=0)


def folded(product):
    return product[:DH] + product[DH:]


def column_scale(value):
    largest = jnp.max(jnp.abs(value), axis=0, keepdims=True)
    return (jnp.maximum(largest, 1e-30) * 1.01).astype(BF16).astype(F32)


def encode(value, scale):
    size = jnp.exp2(jnp.abs(value) * (CODE_SPAN / scale) + CODE_BASE)
    return jnp.where(value < 0, -size, size)


def decode(code, scale):
    size = (jnp.log2(jnp.abs(code)) - CODE_BASE) * (scale / CODE_SPAN)
    return jnp.where(code < 0, -size, size)


def chunk(ref, i, features):
    if ref.shape[1] != features:
        size = ref.shape[0] // CHUNKS
        return ref.at[pl.ds(pl.multiple_of(i * size, size), size), :]
    size = features // CHUNKS
    return ref.at[:, pl.ds(pl.multiple_of(i * size, size), size)]


def rates(rate_ref, index):
    head = lax.broadcasted_iota(jnp.int32, (DH, QUAD), 1) // DH
    value = jnp.full((DH, QUAD), rate_ref[0, index * HEADS], F32)
    for h in range(1, HEADS):
        value = jnp.where(head == h, rate_ref[0, index * HEADS + h], value)
    return value * (1.0 / DH)


def mover(sources, targets, sems, features):
    def copies(i):
        return [
            pltpu.make_async_copy(chunk(source, i, features), chunk(target, i, features), sems.at[n, i])
            for n, (source, target) in enumerate(zip(sources, targets))
        ]

    def start(i):
        for copy in copies(i):
            copy.start()

    def wait(i):
        for copy in copies(i):
            copy.wait()

    return start, wait


def run(work, count, fetch, ship=None, first=None):
    each = count // CHUNKS
    first.start()
    fetch[0](0)
    fetch[0](1)
    first.wait()

    def body(i, carry):
        fetch[1](i)

        @pl.when(i + 2 < CHUNKS)
        def _():
            fetch[0](i + 2)

        for t in range(each):
            index = i * each + t
            work(index, pl.ds(pl.multiple_of(index * QUAD, QUAD), QUAD), t)
        if ship is not None:
            ship[0](i)
        return carry

    lax.fori_loop(0, CHUNKS, body, 0)
    if ship is not None:
        for i in range(CHUNKS):
            ship[1](i)


def map_kernel(rate_hbm, q_hbm, k_hbm, acode_ref, ascale_ref, mt_ref, rate_ref, rate_sem, q_ref, k_ref, in_sems):
    row, col, _ = quad_iota()
    masks = head_masks()
    identity = (row == col).astype(F32).astype(BF16)
    upper = (row <= col).astype(F32)

    def work(index, lanes, t):
        rate = rates(rate_ref, index)
        gates, readouts = [], []
        for b in range(2):
            rows = slice(b * DH, (b + 1) * DH)
            k, q = k_ref[rows, lanes], q_ref[rows, lanes]
            k_block, q_block = diagonal(k, masks), diagonal(q, masks)
            on_q = times_t(both(k, identity), q_block)
            st_hi, st_lo = split(on_q[:DH] * upper)
            qt = on_q[DH:]
            kt = times_t(identity, k_block).astype(BF16)
            gates.append(rate * times(kt, k_block))
            readouts.append(qt - rate * (times(kt, diagonal(st_hi, masks)) + times(kt, diagonal(st_lo, masks))))
        g_hi, g_lo = split(gates[0])
        g_both = both(g_hi, g_lo)

        def gate_times(value):
            hi, lo = split(value)
            return folded(times(g_both, diagonal(hi, masks))) + times(g_hi, diagonal(lo, masks))

        drop = gates[0] + gates[1] - gate_times(gates[1])
        second = readouts[1] - gate_times(readouts[1])
        for b, value in enumerate((readouts[0], second)):
            hi, lo = split(value)
            mt_ref[b * 128 : b * 128 + 64, lanes] = hi
            mt_ref[b * 128 + 64 : b * 128 + 128, lanes] = lo
        scale = column_scale(drop)
        acode_ref[:, lanes] = encode(drop, scale).astype(BF16)
        ascale_ref[:, lanes] = jnp.broadcast_to(scale, (8, QUAD))

    features = k_ref.shape[1]
    fetch = mover((q_hbm, k_hbm), (q_ref, k_ref), in_sems, features)
    run(work, features // QUAD, fetch, None, pltpu.make_async_copy(rate_hbm, rate_ref, rate_sem))


def pack_kernel(mt_ref, dz_ref, acode_ref, ascale_ref, out_ref):
    masks = head_masks()
    left = lax.broadcasted_iota(jnp.int32, (DH, 128), 1) < DH
    left8 = left[:8]

    def work(index, lanes):
        total = folded(times(mt_ref[0:128, lanes], diagonal(dz_ref[0:DH, lanes], masks)))
        total += folded(times(mt_ref[128:256, lanes], diagonal(dz_ref[DH:128, lanes], masks)))
        scale = column_scale(total)
        code = encode(total, scale)
        a_code = acode_ref[:, lanes].astype(F32)
        a_scale = ascale_ref[:, lanes]
        scale = jnp.broadcast_to(scale, (8, QUAD))
        for p in range(PAIRS):
            cut = slice(p * 128, p * 128 + 128)
            head = index * HEADS + p * 2
            out_ref[head, 0:DH, :] = jnp.where(left, a_code[:, cut], pltpu.roll(code[:, cut], DH, 1)).astype(BF16)
            out_ref[head, DH : DH + 8, :] = jnp.where(left8, a_scale[:, cut], pltpu.roll(scale[:, cut], DH, 1)).astype(BF16)
            out_ref[head + 1, 0:DH, :] = jnp.where(left, pltpu.roll(a_code[:, cut], DH, 1), code[:, cut]).astype(BF16)
            out_ref[head + 1, DH : DH + 8, :] = jnp.where(left8, pltpu.roll(a_scale[:, cut], DH, 1), scale[:, cut]).astype(BF16)

    for index in range(dz_ref.shape[1] // QUAD):
        work(index, slice(index * QUAD, (index + 1) * QUAD))


def relay_kernel(in_ref, out_ref, map_ref, left_ref, group):
    shards = in_ref.shape[0]
    row = lax.broadcasted_iota(jnp.int32, (DH, 128), 0)
    lane = lax.broadcasted_iota(jnp.int32, (DH, 128), 1)
    left = lane < DH
    unit = (row == lane).astype(F32)

    def unpack(j, carry):
        scale = in_ref[j, DH : DH + 8, :].astype(F32)[0:1]
        value = decode(in_ref[j, 0:DH, :].astype(F32), scale)
        value = jnp.where(left, unit - value, value)
        map_ref[j] = value
        left_ref[j] = left_operand(value)
        return carry

    def left_operand(value):
        hi, lo = split(value)
        hi_f = hi.astype(F32)
        lo_f = lo.astype(F32)
        first = jnp.where(left, hi_f, pltpu.roll(lo_f, DH, 1)).astype(BF16)
        last = jnp.where(left, hi_f, 0.0).astype(BF16)
        return jnp.concatenate([first, last], axis=1)

    def right_operand(value):
        hi, lo = split(value)
        return jnp.concatenate([hi, hi, lo, jnp.zeros_like(lo)], axis=0)

    lax.fori_loop(0, shards, unpack, 0, unroll=4)
    groups = shards // group
    suffix = [map_ref[g * group + group - 1] for g in range(groups)]
    for step in range(group - 2, -1, -1):
        for g in range(groups):
            j = g * group + step
            own = map_ref[j]
            suffix[g] = times(left_ref[j], right_operand(suffix[g])) + jnp.where(left, 0.0, own)
            map_ref[j] = suffix[g]
            left_ref[j] = left_operand(suffix[g])
    ends = [None] * groups
    ends[groups - 1] = jnp.zeros((DH, 128), F32)
    for g in range(groups - 2, -1, -1):
        j = (g + 1) * group
        ends[g] = times(left_ref[j], right_operand(ends[g + 1])) + map_ref[j]
    for g in range(groups):
        right = right_operand(ends[g])
        found = []
        for step in range(group):
            j = g * group + step
            if step == group - 1:
                found.append(ends[g])
            else:
                found.append(times(left_ref[j + 1], right) + map_ref[j + 1])
        for step in range(0, group, 2):
            pair = jnp.where(left, pltpu.roll(found[step], DH, 1), found[step + 1])
            scale = column_scale(pair)
            code = encode(pair, scale)
            turned = pltpu.roll(code, DH, 1)
            scale = jnp.broadcast_to(scale, (8, 128))
            j = g * group + step
            half = DH // 2
            low = left[:half]
            out_ref[j, 0:half, :] = jnp.where(low, code[:half], turned[half:]).astype(BF16)
            other = pltpu.roll(scale, DH, 1)
            out_ref[j, half : half + 8, :] = jnp.where(left[:8], scale, other).astype(BF16)
            out_ref[j + 1, 0:half, :] = jnp.where(low, turned[:half], code[half:]).astype(BF16)
            out_ref[j + 1, half : half + 8, :] = jnp.where(left[:8], other, scale).astype(BF16)


def trail_kernel(rate_hbm, *refs):
    inputs, (e_ref, wt_ref), outputs, (rate_ref, rate_sem) = refs[:5], refs[5:7], refs[7:10], refs[10:12]
    q_ref, k_ref, v_ref, w_ref, dz_ref = refs[12:17]
    kt_ref, t_ref, outer_ref = refs[17:20]
    flat_ref, in_sems, out_sems = refs[20:]
    row, col, _ = quad_iota()
    masks = head_masks()
    identity = (row == col).astype(F32).astype(BF16)
    upper = (row <= col).astype(F32)
    half = DH // 2
    low = lax.broadcasted_iota(jnp.int32, (half, 128), 1) < DH

    def start_weight(pair):
        first = pl.multiple_of(pair * DH, DH)
        one = flat_ref[pl.ds(first, half), :]
        two = flat_ref[pl.ds(first + half, half), :]
        even = jnp.where(low, one, pltpu.roll(two, DH, 1))
        odd = jnp.where(low, pltpu.roll(one, DH, 1), two)
        flat_ref[pl.ds(first, half, stride=2), :] = even
        flat_ref[pl.ds(first + 1, half, stride=2), :] = odd
        return flat_ref[pl.ds(first, DH), :]

    def work(index, lanes, t):
        rate = rates(rate_ref, index)
        if t == 0:
            first = pl.multiple_of(index * HEADS, 8)
            for i in range(half):
                flat_ref[pl.ds(first * half + i, 8, stride=half), :] = w_ref[pl.ds(first, 8), i * 128 : (i + 1) * 128]
        weight = jnp.concatenate([start_weight(index * PAIRS + p) for p in range(PAIRS)], axis=1)
        for b in range(2):
            rows = slice(b * DH, (b + 1) * DH)
            hi_rows, lo_rows = slice(b * 128, b * 128 + 64), slice(b * 128 + 64, b * 128 + 128)
            k = k_ref[rows, lanes]
            w_hi, w_lo = split(weight)
            wt_ref[hi_rows, lanes] = w_hi
            wt_ref[lo_rows, lanes] = w_lo
            error = times(k, diagonal(w_hi, masks)) + times(k, diagonal(w_lo, masks)) - v_ref[rows, lanes].astype(F32)
            e_hi, e_lo = split(error)
            e_ref[hi_rows, lanes] = e_hi
            e_ref[lo_rows, lanes] = e_lo
            kt = times_t(identity, diagonal(k, masks)).astype(BF16)
            kt_ref[rows, lanes] = kt
            if b == 0:
                weight = weight - rate * (times(kt, diagonal(e_hi, masks)) + times(kt, diagonal(e_lo, masks)))
            on_q = times_t(both(k, identity), diagonal(q_ref[rows, lanes], masks))
            st_hi, st_lo = split(on_q[:DH] * upper)
            qt = on_q[DH:].astype(BF16)
            on_dz = times(jnp.concatenate([st_hi, st_lo, qt], axis=0), diagonal(dz_ref[rows, lanes], masks))
            t_ref[rows, lanes] = on_dz[:DH] + on_dz[DH:128]
            outer_ref[rows, lanes] = on_dz[128:]

    features = k_ref.shape[1]
    fetch = mover(inputs, refs[12:17], in_sems, features)
    ship = mover(refs[17:20], outputs, out_sems, features)
    run(work, features // QUAD, fetch, ship, pltpu.make_async_copy(rate_hbm, rate_ref, rate_sem))


def direct_kernel(rate_hbm, e_ref, wt_ref, *refs):
    inputs, outputs, (rate_ref, rate_sem) = refs[:3], refs[3:5], refs[5:7]
    q_ref, k_ref, dz_ref, gq_ref, part_ref, in_sems, out_sems = refs[7:]
    row, col, _ = quad_iota()
    masks = head_masks()
    upper = (row <= col).astype(F32)
    lower = (row >= col).astype(F32)

    def work(index, lanes, t):
        rate = rates(rate_ref, index)
        for b in range(2):
            rows = slice(b * DH, (b + 1) * DH)
            two = slice(b * 128, b * 128 + 128)
            hi_rows, lo_rows = slice(b * 128, b * 128 + 64), slice(b * 128 + 64, b * 128 + 128)
            dz = dz_ref[rows, lanes]
            dpt = folded(times_t(e_ref[two, lanes], diagonal(dz, masks))) * (-rate * upper)
            dp = times_t(dz, diagonal(e_ref[hi_rows, lanes], masks)) + times_t(dz, diagonal(e_ref[lo_rows, lanes], masks))
            dp = dp * (-rate * lower)
            grad = times_t(dz, diagonal(wt_ref[hi_rows, lanes], masks)) + times_t(dz, diagonal(wt_ref[lo_rows, lanes], masks))
            grad += folded(times(both(*split(dp)), diagonal(k_ref[rows, lanes], masks)))
            gq_ref[rows, lanes] = grad.astype(BF16)
            part_ref[rows, lanes] = folded(times(both(*split(dpt)), diagonal(q_ref[rows, lanes], masks)))

    features = k_ref.shape[1]
    fetch = mover(inputs, (q_ref, k_ref, dz_ref), in_sems, features)
    ship = mover((gq_ref, part_ref), outputs, out_sems, features)
    run(work, features // QUAD, fetch, ship, pltpu.make_async_copy(rate_hbm, rate_ref, rate_sem))


def final_kernel(rate_hbm, code_ref, e_ref, wt_ref, *refs):
    inputs, outputs, (rate_ref, rate_sem) = refs[:5], refs[5:8], refs[8:10]
    k_ref, kt_ref, t_ref, outer_ref, part_ref = refs[10:15]
    gk_ref, gv_ref, start_ref, flat_ref, in_sems, out_sems = refs[15:]
    masks = head_masks()
    half = DH // 2
    low = lax.broadcasted_iota(jnp.int32, (half, 128), 1) < DH

    def work(index, lanes, t):
        rate = rates(rate_ref, index)
        pairs = []
        for p in range(PAIRS):
            halves = []
            for h in range(2):
                head = index * HEADS + p * 2 + h
                scale = code_ref[head, half : half + 8, :].astype(F32)[0:1]
                halves.append(decode(code_ref[head, 0:half, :].astype(F32), scale))
            top = jnp.where(low, halves[0], pltpu.roll(halves[1], DH, 1))
            bottom = jnp.where(low, pltpu.roll(halves[0], DH, 1), halves[1])
            pairs.append(jnp.concatenate([top, bottom], axis=0))
        adjoint = jnp.concatenate(pairs, axis=1)
        for b in (1, 0):
            rows = slice(b * DH, (b + 1) * DH)
            two = slice(b * 128, b * 128 + 128)
            hi_rows, lo_rows = slice(b * 128, b * 128 + 64), slice(b * 128 + 64, b * 128 + 128)
            g_hi, g_lo = split(adjoint)
            g_block, g_low_block = diagonal(g_hi, masks), diagonal(g_lo, masks)
            k = k_ref[rows, lanes]
            slope = t_ref[rows, lanes] + times(k, g_block) + times(k, g_low_block)
            grad_error = -rate * slope
            gv_ref[rows, lanes] = (-grad_error).astype(BF16)
            d_hi, d_lo = split(grad_error)
            kt = kt_ref[rows, lanes]
            grad = part_ref[rows, lanes]
            grad += folded(times_t(both(d_hi, d_lo), diagonal(wt_ref[hi_rows, lanes], masks)))
            grad += times_t(d_hi, diagonal(wt_ref[lo_rows, lanes], masks))
            on_g = folded(times_t(e_ref[two, lanes], g_block)) + times_t(e_ref[hi_rows, lanes], g_low_block)
            gk_ref[rows, lanes] = (grad - rate * on_g).astype(BF16)
            adjoint = adjoint + outer_ref[rows, lanes] + times(kt, diagonal(d_hi, masks)) + times(kt, diagonal(d_lo, masks))
        for p in range(PAIRS):
            first = pl.multiple_of((index * PAIRS + p) * DH, DH)
            flat_ref[pl.ds(first, DH), :] = adjoint[:, p * 128 : p * 128 + 128]
            even = flat_ref[pl.ds(first, half, stride=2), :]
            odd = flat_ref[pl.ds(first + 1, half, stride=2), :]
            flat_ref[pl.ds(first, half), :] = jnp.where(low, even, pltpu.roll(odd, DH, 1))
            flat_ref[pl.ds(first + half, half), :] = jnp.where(low, pltpu.roll(even, DH, 1), odd)
        if (t + 1) * HEADS == 8:
            head = pl.multiple_of((index + 1) * HEADS - 8, 8)
            for i in range(half):
                start_ref[pl.ds(head, 8), i * 128 : (i + 1) * 128] = flat_ref[pl.ds(head * half + i, 8, stride=half), :]

    features = k_ref.shape[1]
    fetch = mover(inputs, refs[10:15], in_sems, features)
    ship = mover((gk_ref, gv_ref, start_ref), outputs, out_sems, features)
    run(work, features // QUAD, fetch, ship, pltpu.make_async_copy(rate_hbm, rate_ref, rate_sem))


def call(kernel, ins, outs, flops, scratch=(), limit=58):
    args = [array for array, _ in ins]
    size = sum(a.size * a.dtype.itemsize for a in args) + sum(o.size * o.dtype.itemsize for o, _ in outs)
    return pl.pallas_call(
        kernel,
        out_shape=tuple(shape if memory is pltpu.VMEM else pltpu.HBM(shape.shape, shape.dtype) for shape, memory in outs),
        in_specs=[pl.BlockSpec(memory_space=memory) for _, memory in ins],
        out_specs=tuple(pl.BlockSpec(memory_space=memory) for _, memory in outs),
        scratch_shapes=list(scratch),
        compiler_params=pltpu.CompilerParams(vmem_limit_bytes=limit * 1024 * 1024),
        cost_estimate=pl.CostEstimate(flops=flops, bytes_accessed=size, transcendentals=0),
    )(*args)


def per_device(queries, memory_keys, memory_values, upstream, inner_rate, checkpoints):
    sections = lax.axis_size("section")
    shards = lax.axis_size("seq")
    heads = inner_rate.shape[1]
    features = queries.shape[2]
    tokens = queries.shape[1]
    q, k, v, w = queries[0], memory_keys[0], memory_values[0], checkpoints[0, 0]

    def array(rows, kind, columns=features):
        return jax.ShapeDtypeStruct((rows, columns), kind)

    def apart(a):
        return jax.ShapeDtypeStruct((a.shape[0] * CHUNKS, a.shape[1] // CHUNKS), a.dtype)

    def buffers(arrays):
        return [pltpu.VMEM(a.shape, a.dtype) for a in arrays]

    def semaphores(count):
        return pltpu.SemaphoreType.DMA((count, CHUNKS))

    def outside(arrays):
        return [(a if isinstance(a, jax.ShapeDtypeStruct) else pltpu.with_memory_space_constraint(a, pltpu.HBM), pltpu.HBM) for a in arrays]

    def inside(arrays):
        return [(a, pltpu.VMEM) for a in arrays]

    unit = 2 * tokens * features * QUAD
    flat = pltpu.VMEM((heads * DH // 2, 128), F32)
    single, whole, double = array(tokens, F32), array(tokens, BF16), array(2 * tokens, BF16)
    rate = [pltpu.SMEM(inner_rate.shape, F32), pltpu.SemaphoreType.DMA]

    cotangent = lax.ppermute(upstream, "section", [((i + 1) % sections, i) for i in range(sections)])
    dz = cotangent[0]
    acode, ascale, mt = call(
        map_kernel,
        outside([inner_rate, q, k]),
        inside([array(DH, BF16), array(8, F32), double]),
        8 * unit,
        rate + buffers([q, k]) + [semaphores(2)],
        MAP_LIMIT,
    )
    (packed,) = call(
        pack_kernel, inside([mt, dz, acode, ascale]), inside([jax.ShapeDtypeStruct((heads, DH + 8, 128), BF16)]), 2 * unit, (), 24
    )
    arrived = lax.all_to_all(packed, "seq", 0, 0, tiled=True)
    rate_later, _ = lax.optimization_barrier((inner_rate, packed))
    given, made = [q, k, v, w, dz], [whole, single, single]
    error, weights, kt, slope, outer = call(
        trail_kernel,
        outside([rate_later] + given),
        inside([double, double]) + outside([apart(a) for a in made]),
        10 * unit,
        rate + buffers(given + made) + [flat, semaphores(5), semaphores(3)],
        LATE_LIMIT,
    )
    arrived, slope = lax.optimization_barrier((arrived, slope))
    (ends,) = call(
        partial(relay_kernel, group=8),
        inside([arrived]),
        inside([jax.ShapeDtypeStruct((shards, DH // 2 + 8, 128), BF16)]),
        unit,
        [pltpu.VMEM((shards, DH, 128), F32), pltpu.VMEM((shards, DH, 256), BF16)],
        24,
    )
    returned = lax.all_to_all(ends, "seq", 0, 0, tiled=True)
    rate_later, _ = lax.optimization_barrier((inner_rate, ends))
    grad_q, part = call(
        direct_kernel,
        outside([rate_later]) + inside([error, weights]) + outside([q, k, dz]),
        outside([whole, apart(single)]),
        10 * unit,
        rate + buffers([whole, whole, whole, whole, single]) + [semaphores(3), semaphores(2)],
        LATE_LIMIT,
    )
    held, made = [whole, whole, single, single, single], [whole, whole, array(heads, F32, DH * DH)]
    grad_k, grad_v, start = call(
        final_kernel,
        outside([inner_rate]) + inside([returned, error, weights]) + outside([k, kt, slope, outer, part]),
        outside(made),
        10 * unit,
        rate + buffers(held + made) + [flat, semaphores(5), semaphores(3)],
        LATE_LIMIT,
    )
    return grad_q[None], grad_k[None], grad_v[None], start[None, None]


def solution(mesh):
    tokens = P("section", "seq", None)
    return jax.shard_map(
        per_device,
        mesh=mesh,
        in_specs=(tokens, tokens, tokens, tokens, P("section", None), P("section", "seq", None, None)),
        out_specs=(tokens, tokens, tokens, P("section", "seq", None, None)),
        check_vma=False,
    )
```

```python
from functools import partial

import jax
import jax.numpy as jnp
from jax import lax
from jax.experimental import pallas as pl
from jax.experimental.pallas import tpu as pltpu
from jax.sharding import PartitionSpec as P

DH = 64
QUAD = 4 * DH
PAIRS = QUAD // 128
HEADS = QUAD // DH
F32 = jnp.float32
BF16 = jnp.bfloat16
CHUNKS = 4
MAP_LIMIT = 24
LATE_LIMIT = 24
CODE_SPAN = 250.0
CODE_BASE = -125.0


def quad_iota():
    row = lax.broadcasted_iota(jnp.int32, (DH, QUAD), 0)
    lane = lax.broadcasted_iota(jnp.int32, (DH, QUAD), 1)
    return row, lane % DH, lane // DH


def head_masks():
    head = quad_iota()[2]
    return [(head == h).astype(F32).astype(BF16) for h in range(QUAD // DH)]


def diagonal(right, masks):
    return jnp.concatenate([right * mask for mask in masks], axis=0)


def times(left, block):
    return lax.dot_general(left, block, (((1,), (0,)), ((), ())), preferred_element_type=F32)


def times_t(left, block):
    return lax.dot_general(left, block, (((1,), (1,)), ((), ())), preferred_element_type=F32)


def split(value):
    high = value.astype(BF16)
    low = (value - high.astype(F32)).astype(BF16)
    return high, low


def both(high, low):
    return jnp.concatenate([high, low], axis=0)


def folded(product):
    return product[:DH] + product[DH:]


def column_scale(value):
    largest = jnp.max(jnp.abs(value), axis=0, keepdims=True)
    return (jnp.maximum(largest, 1e-30) * 1.01).astype(BF16).astype(F32)


def encode(value, scale):
    size = jnp.exp2(jnp.abs(value) * (CODE_SPAN / scale) + CODE_BASE)
    return jnp.where(value < 0, -size, size)


def decode(code, scale):
    size = (jnp.log2(jnp.abs(code)) - CODE_BASE) * (scale / CODE_SPAN)
    return jnp.where(code < 0, -size, size)


def chunk(ref, i, features):
    if ref.shape[1] != features:
        size = ref.shape[0] // CHUNKS
        return ref.at[pl.ds(pl.multiple_of(i * size, size), size), :]
    size = features // CHUNKS
    return ref.at[:, pl.ds(pl.multiple_of(i * size, size), size)]


def rates(rate_ref, index):
    head = lax.broadcasted_iota(jnp.int32, (DH, QUAD), 1) // DH
    value = jnp.full((DH, QUAD), rate_ref[0, index * HEADS], F32)
    for h in range(1, HEADS):
        value = jnp.where(head == h, rate_ref[0, index * HEADS + h], value)
    return value * (1.0 / DH)


def mover(sources, targets, sems, features):
    def copies(i):
        return [
            pltpu.make_async_copy(chunk(source, i, features), chunk(target, i, features), sems.at[n, i])
            for n, (source, target) in enumerate(zip(sources, targets))
        ]

    def start(i):
        for copy in copies(i):
            copy.start()

    def wait(i):
        for copy in copies(i):
            copy.wait()

    return start, wait


def run(work, count, fetch, ship=None, first=None):
    each = count // CHUNKS
    first.start()
    fetch[0](0)
    fetch[0](1)
    first.wait()

    def body(i, carry):
        fetch[1](i)

        @pl.when(i + 2 < CHUNKS)
        def _():
            fetch[0](i + 2)

        for t in range(each):
            index = i * each + t
            work(index, pl.ds(pl.multiple_of(index * QUAD, QUAD), QUAD), t)
        if ship is not None:
            ship[0](i)
        return carry

    lax.fori_loop(0, CHUNKS, body, 0)
    if ship is not None:
        for i in range(CHUNKS):
            ship[1](i)


def map_kernel(rate_hbm, q_hbm, k_hbm, acode_ref, ascale_ref, mt_ref, rate_ref, rate_sem, q_ref, k_ref, in_sems):
    row, col, _ = quad_iota()
    masks = head_masks()
    identity = (row == col).astype(F32).astype(BF16)
    upper = (row <= col).astype(F32)

    def work(index, lanes, t):
        rate = rates(rate_ref, index)
        gates, readouts = [], []
        for b in range(2):
            rows = slice(b * DH, (b + 1) * DH)
            k, q = k_ref[rows, lanes], q_ref[rows, lanes]
            k_block, q_block = diagonal(k, masks), diagonal(q, masks)
            on_q = times_t(both(k, identity), q_block)
            st_hi, st_lo = split(on_q[:DH] * upper)
            qt = on_q[DH:]
            kt = times_t(identity, k_block).astype(BF16)
            gates.append(rate * times(kt, k_block))
            readouts.append(qt - rate * (times(kt, diagonal(st_hi, masks)) + times(kt, diagonal(st_lo, masks))))
        g_hi, g_lo = split(gates[0])
        g_both = both(g_hi, g_lo)

        def gate_times(value):
            hi, lo = split(value)
            return folded(times(g_both, diagonal(hi, masks))) + times(g_hi, diagonal(lo, masks))

        drop = gates[0] + gates[1] - gate_times(gates[1])
        second = readouts[1] - gate_times(readouts[1])
        for b, value in enumerate((readouts[0], second)):
            hi, lo = split(value)
            mt_ref[b * 128 : b * 128 + 64, lanes] = hi
            mt_ref[b * 128 + 64 : b * 128 + 128, lanes] = lo
        scale = column_scale(drop)
        acode_ref[:, lanes] = encode(drop, scale).astype(BF16)
        ascale_ref[:, lanes] = jnp.broadcast_to(scale, (8, QUAD))

    features = k_ref.shape[1]
    fetch = mover((q_hbm, k_hbm), (q_ref, k_ref), in_sems, features)
    run(work, features // QUAD, fetch, None, pltpu.make_async_copy(rate_hbm, rate_ref, rate_sem))


def pack_kernel(mt_ref, dz_ref, acode_ref, ascale_ref, out_ref):
    masks = head_masks()
    left = lax.broadcasted_iota(jnp.int32, (DH, 128), 1) < DH
    left8 = left[:8]

    def work(index, lanes):
        total = folded(times(mt_ref[0:128, lanes], diagonal(dz_ref[0:DH, lanes], masks)))
        total += folded(times(mt_ref[128:256, lanes], diagonal(dz_ref[DH:128, lanes], masks)))
        scale = column_scale(total)
        code = encode(total, scale)
        a_code = acode_ref[:, lanes].astype(F32)
        a_scale = ascale_ref[:, lanes]
        scale = jnp.broadcast_to(scale, (8, QUAD))
        for p in range(PAIRS):
            cut = slice(p * 128, p * 128 + 128)
            head = index * HEADS + p * 2
            out_ref[head, 0:DH, :] = jnp.where(left, a_code[:, cut], pltpu.roll(code[:, cut], DH, 1)).astype(BF16)
            out_ref[head, DH : DH + 8, :] = jnp.where(left8, a_scale[:, cut], pltpu.roll(scale[:, cut], DH, 1)).astype(BF16)
            out_ref[head + 1, 0:DH, :] = jnp.where(left, pltpu.roll(a_code[:, cut], DH, 1), code[:, cut]).astype(BF16)
            out_ref[head + 1, DH : DH + 8, :] = jnp.where(left8, pltpu.roll(a_scale[:, cut], DH, 1), scale[:, cut]).astype(BF16)

    for index in range(dz_ref.shape[1] // QUAD):
        work(index, slice(index * QUAD, (index + 1) * QUAD))


def relay_kernel(in_ref, out_ref, map_ref, left_ref, group):
    shards = in_ref.shape[0]
    row = lax.broadcasted_iota(jnp.int32, (DH, 128), 0)
    lane = lax.broadcasted_iota(jnp.int32, (DH, 128), 1)
    left = lane < DH
    unit = (row == lane).astype(F32)

    def unpack(j):
        scale = in_ref[j, DH : DH + 8, :].astype(F32)[0:1]
        value = decode(in_ref[j, 0:DH, :].astype(F32), scale)
        return jnp.where(left, unit - value, value)

    def left_operand(value):
        hi, lo = split(value)
        hi_f = hi.astype(F32)
        lo_f = lo.astype(F32)
        first = jnp.where(left, hi_f, pltpu.roll(lo_f, DH, 1)).astype(BF16)
        last = jnp.where(left, hi_f, 0.0).astype(BF16)
        return jnp.concatenate([first, last], axis=1)

    def right_operand(value):
        hi, lo = split(value)
        return jnp.concatenate([hi, hi, lo, jnp.zeros_like(lo)], axis=0)

    groups = shards // group
    suffix = []
    for g in range(groups):
        j = g * group + group - 1
        suffix.append(unpack(j))
        map_ref[j] = suffix[g]
        left_ref[j] = left_operand(suffix[g])
    for step in range(group - 2, -1, -1):
        for g in range(groups):
            j = g * group + step
            own = unpack(j)
            suffix[g] = times(left_operand(own), right_operand(suffix[g])) + jnp.where(left, 0.0, own)
            map_ref[j] = suffix[g]
            left_ref[j] = left_operand(suffix[g])
    ends = [None] * groups
    ends[groups - 1] = jnp.zeros((DH, 128), F32)
    for g in range(groups - 2, -1, -1):
        j = (g + 1) * group
        ends[g] = times(left_ref[j], right_operand(ends[g + 1])) + map_ref[j]
    for g in range(groups):
        right = right_operand(ends[g])
        found = []
        for step in range(group):
            j = g * group + step
            if step == group - 1:
                found.append(ends[g])
            else:
                found.append(times(left_ref[j + 1], right) + map_ref[j + 1])
        for step in range(0, group, 2):
            pair = jnp.where(left, pltpu.roll(found[step], DH, 1), found[step + 1])
            scale = column_scale(pair)
            code = encode(pair, scale)
            turned = pltpu.roll(code, DH, 1)
            scale = jnp.broadcast_to(scale, (8, 128))
            j = g * group + step
            half = DH // 2
            low = left[:half]
            out_ref[j, 0:half, :] = jnp.where(low, code[:half], turned[half:]).astype(BF16)
            other = pltpu.roll(scale, DH, 1)
            out_ref[j, half : half + 8, :] = jnp.where(left[:8], scale, other).astype(BF16)
            out_ref[j + 1, 0:half, :] = jnp.where(low, turned[:half], code[half:]).astype(BF16)
            out_ref[j + 1, half : half + 8, :] = jnp.where(left[:8], other, scale).astype(BF16)


def trail_kernel(rate_hbm, *refs):
    inputs, (e_ref, wt_ref), outputs, (rate_ref, rate_sem) = refs[:5], refs[5:7], refs[7:10], refs[10:12]
    q_ref, k_ref, v_ref, w_ref, dz_ref = refs[12:17]
    gate_ref, t_ref, source_ref = refs[17:20]
    flat_ref, in_sems, out_sems = refs[20:]
    row, col, _ = quad_iota()
    masks = head_masks()
    identity = (row == col).astype(F32).astype(BF16)
    upper = (row <= col).astype(F32)
    half = DH // 2
    low = lax.broadcasted_iota(jnp.int32, (half, 128), 1) < DH

    def start_weight(pair):
        first = pl.multiple_of(pair * DH, DH)
        one = flat_ref[pl.ds(first, half), :]
        two = flat_ref[pl.ds(first + half, half), :]
        even = jnp.where(low, one, pltpu.roll(two, DH, 1))
        odd = jnp.where(low, pltpu.roll(one, DH, 1), two)
        flat_ref[pl.ds(first, half, stride=2), :] = even
        flat_ref[pl.ds(first + 1, half, stride=2), :] = odd
        return flat_ref[pl.ds(first, DH), :]

    def work(index, lanes, t):
        rate = rates(rate_ref, index)
        if t == 0:
            first = pl.multiple_of(index * HEADS, 8)
            for i in range(half):
                flat_ref[pl.ds(first * half + i, 8, stride=half), :] = w_ref[pl.ds(first, 8), i * 128 : (i + 1) * 128]
        weight = jnp.concatenate([start_weight(index * PAIRS + p) for p in range(PAIRS)], axis=1)
        for b in range(2):
            rows = slice(b * DH, (b + 1) * DH)
            hi_rows, lo_rows = slice(b * 128, b * 128 + 64), slice(b * 128 + 64, b * 128 + 128)
            k = k_ref[rows, lanes]
            w_hi, w_lo = split(weight)
            w_block, w_low_block = diagonal(w_hi, masks), diagonal(w_lo, masks)
            wt_ref[hi_rows, lanes] = times_t(identity, w_block).astype(BF16)
            wt_ref[lo_rows, lanes] = times_t(identity, w_low_block).astype(BF16)
            error = times(k, w_block) + times(k, w_low_block) - v_ref[rows, lanes].astype(F32)
            e_hi, e_lo = split(error)
            e_ref[hi_rows, lanes] = e_hi
            e_ref[lo_rows, lanes] = e_lo
            k_block = diagonal(k, masks)
            kt = times_t(identity, k_block).astype(BF16)
            gate_hi, gate_lo = split(rate * times(kt, k_block))
            gate_ref[hi_rows, lanes] = gate_hi
            gate_ref[lo_rows, lanes] = gate_lo
            if b == 0:
                weight = weight - rate * (times(kt, diagonal(e_hi, masks)) + times(kt, diagonal(e_lo, masks)))
            on_q = times_t(both(k, identity), diagonal(q_ref[rows, lanes], masks))
            st_hi, st_lo = split(on_q[:DH] * upper)
            qt = on_q[DH:].astype(BF16)
            on_dz = times(jnp.concatenate([st_hi, st_lo, qt], axis=0), diagonal(dz_ref[rows, lanes], masks))
            slope = on_dz[:DH] + on_dz[DH:128]
            t_ref[rows, lanes] = slope
            t_hi, t_lo = split(slope)
            source_ref[rows, lanes] = on_dz[128:] - rate * (times(kt, diagonal(t_hi, masks)) + times(kt, diagonal(t_lo, masks)))

    features = k_ref.shape[1]
    fetch = mover(inputs, refs[12:17], in_sems, features)
    ship = mover(refs[17:20], outputs, out_sems, features)
    run(work, features // QUAD, fetch, ship, pltpu.make_async_copy(rate_hbm, rate_ref, rate_sem))


def direct_kernel(rate_hbm, e_ref, wt_ref, *refs):
    inputs, outputs, (rate_ref, rate_sem) = refs[:3], refs[3:5], refs[5:7]
    q_ref, k_ref, dz_ref, gq_ref, part_ref, in_sems, out_sems = refs[7:]
    row, col, _ = quad_iota()
    masks = head_masks()
    upper = (row <= col).astype(F32)
    lower = (row >= col).astype(F32)

    def work(index, lanes, t):
        rate = rates(rate_ref, index)
        for b in range(2):
            rows = slice(b * DH, (b + 1) * DH)
            two = slice(b * 128, b * 128 + 128)
            hi_rows, lo_rows = slice(b * 128, b * 128 + 64), slice(b * 128 + 64, b * 128 + 128)
            dz = dz_ref[rows, lanes]
            dpt = folded(times_t(e_ref[two, lanes], diagonal(dz, masks))) * (-rate * upper)
            dp = times_t(dz, diagonal(e_ref[hi_rows, lanes], masks)) + times_t(dz, diagonal(e_ref[lo_rows, lanes], masks))
            dp = dp * (-rate * lower)
            grad = times(dz, diagonal(wt_ref[hi_rows, lanes], masks)) + times(dz, diagonal(wt_ref[lo_rows, lanes], masks))
            grad += folded(times(both(*split(dp)), diagonal(k_ref[rows, lanes], masks)))
            gq_ref[rows, lanes] = grad.astype(BF16)
            part_ref[rows, lanes] = folded(times(both(*split(dpt)), diagonal(q_ref[rows, lanes], masks)))

    features = k_ref.shape[1]
    fetch = mover(inputs, (q_ref, k_ref, dz_ref), in_sems, features)
    ship = mover((gq_ref, part_ref), outputs, out_sems, features)
    run(work, features // QUAD, fetch, ship, pltpu.make_async_copy(rate_hbm, rate_ref, rate_sem))


def final_kernel(rate_hbm, code_ref, e_ref, wt_ref, *refs):
    inputs, outputs, (rate_ref, rate_sem) = refs[:5], refs[5:8], refs[8:10]
    k_ref, gate_ref, t_ref, source_ref, part_ref = refs[10:15]
    gk_ref, gv_ref, start_ref, flat_ref, in_sems, out_sems = refs[15:]
    masks = head_masks()
    half = DH // 2
    low = lax.broadcasted_iota(jnp.int32, (half, 128), 1) < DH

    def work(index, lanes, t):
        rate = rates(rate_ref, index)
        pairs = []
        for p in range(PAIRS):
            halves = []
            for h in range(2):
                head = index * HEADS + p * 2 + h
                scale = code_ref[head, half : half + 8, :].astype(F32)[0:1]
                halves.append(decode(code_ref[head, 0:half, :].astype(F32), scale))
            top = jnp.where(low, halves[0], pltpu.roll(halves[1], DH, 1))
            bottom = jnp.where(low, pltpu.roll(halves[0], DH, 1), halves[1])
            pairs.append(jnp.concatenate([top, bottom], axis=0))
        adjoint = jnp.concatenate(pairs, axis=1)
        for b in (1, 0):
            rows = slice(b * DH, (b + 1) * DH)
            two = slice(b * 128, b * 128 + 128)
            hi_rows, lo_rows = slice(b * 128, b * 128 + 64), slice(b * 128 + 64, b * 128 + 128)
            g_hi, g_lo = split(adjoint)
            g_block, g_low_block = diagonal(g_hi, masks), diagonal(g_lo, masks)
            k, gate = k_ref[rows, lanes], gate_ref[two, lanes]
            high = times(jnp.concatenate([k, gate], axis=0), g_block)
            low_part = times(jnp.concatenate([k, gate[:DH]], axis=0), g_low_block)
            slope = t_ref[rows, lanes] + high[:DH] + low_part[:DH]
            adjoint = adjoint - (folded(high[DH:]) + low_part[DH:]) + source_ref[rows, lanes]
            grad_error = -rate * slope
            gv_ref[rows, lanes] = (-grad_error).astype(BF16)
            d_hi, d_lo = split(grad_error)
            grad = part_ref[rows, lanes]
            grad += folded(times(both(d_hi, d_lo), diagonal(wt_ref[hi_rows, lanes], masks)))
            grad += times(d_hi, diagonal(wt_ref[lo_rows, lanes], masks))
            on_g = folded(times_t(e_ref[two, lanes], g_block)) + times_t(e_ref[hi_rows, lanes], g_low_block)
            gk_ref[rows, lanes] = (grad - rate * on_g).astype(BF16)
        for p in range(PAIRS):
            first = pl.multiple_of((index * PAIRS + p) * DH, DH)
            flat_ref[pl.ds(first, DH), :] = adjoint[:, p * 128 : p * 128 + 128]
            even = flat_ref[pl.ds(first, half, stride=2), :]
            odd = flat_ref[pl.ds(first + 1, half, stride=2), :]
            flat_ref[pl.ds(first, half), :] = jnp.where(low, even, pltpu.roll(odd, DH, 1))
            flat_ref[pl.ds(first + half, half), :] = jnp.where(low, pltpu.roll(even, DH, 1), odd)
        if (t + 1) * HEADS == 8:
            head = pl.multiple_of((index + 1) * HEADS - 8, 8)
            for i in range(half):
                start_ref[pl.ds(head, 8), i * 128 : (i + 1) * 128] = flat_ref[pl.ds(head * half + i, 8, stride=half), :]

    features = k_ref.shape[1]
    fetch = mover(inputs, refs[10:15], in_sems, features)
    ship = mover((gk_ref, gv_ref, start_ref), outputs, out_sems, features)
    run(work, features // QUAD, fetch, ship, pltpu.make_async_copy(rate_hbm, rate_ref, rate_sem))


def call(kernel, ins, outs, flops, scratch=(), limit=58):
    args = [array for array, _ in ins]
    size = sum(a.size * a.dtype.itemsize for a in args) + sum(o.size * o.dtype.itemsize for o, _ in outs)
    return pl.pallas_call(
        kernel,
        out_shape=tuple(shape if memory is pltpu.VMEM else pltpu.HBM(shape.shape, shape.dtype) for shape, memory in outs),
        in_specs=[pl.BlockSpec(memory_space=memory) for _, memory in ins],
        out_specs=tuple(pl.BlockSpec(memory_space=memory) for _, memory in outs),
        scratch_shapes=list(scratch),
        compiler_params=pltpu.CompilerParams(vmem_limit_bytes=limit * 1024 * 1024),
        cost_estimate=pl.CostEstimate(flops=flops, bytes_accessed=size, transcendentals=0),
    )(*args)


def per_device(queries, memory_keys, memory_values, upstream, inner_rate, checkpoints):
    sections = lax.axis_size("section")
    shards = lax.axis_size("seq")
    heads = inner_rate.shape[1]
    features = queries.shape[2]
    tokens = queries.shape[1]
    q, k, v, w = queries[0], memory_keys[0], memory_values[0], checkpoints[0, 0]

    def array(rows, kind, columns=features):
        return jax.ShapeDtypeStruct((rows, columns), kind)

    def apart(a):
        return jax.ShapeDtypeStruct((a.shape[0] * CHUNKS, a.shape[1] // CHUNKS), a.dtype)

    def buffers(arrays):
        return [pltpu.VMEM(a.shape, a.dtype) for a in arrays]

    def semaphores(count):
        return pltpu.SemaphoreType.DMA((count, CHUNKS))

    def outside(arrays):
        return [(a if isinstance(a, jax.ShapeDtypeStruct) else pltpu.with_memory_space_constraint(a, pltpu.HBM), pltpu.HBM) for a in arrays]

    def inside(arrays):
        return [(a, pltpu.VMEM) for a in arrays]

    unit = 2 * tokens * features * QUAD
    flat = pltpu.VMEM((heads * DH // 2, 128), F32)
    single, whole, double = array(tokens, F32), array(tokens, BF16), array(2 * tokens, BF16)
    rate = [pltpu.SMEM(inner_rate.shape, F32), pltpu.SemaphoreType.DMA]

    cotangent = lax.ppermute(upstream, "section", [((i + 1) % sections, i) for i in range(sections)])
    dz = cotangent[0]
    acode, ascale, mt = call(
        map_kernel,
        outside([inner_rate, q, k]),
        inside([array(DH, BF16), array(8, F32), double]),
        8 * unit,
        rate + buffers([q, k]) + [semaphores(2)],
        MAP_LIMIT,
    )
    (packed,) = call(
        pack_kernel, inside([mt, dz, acode, ascale]), inside([jax.ShapeDtypeStruct((heads, DH + 8, 128), BF16)]), 2 * unit, (), 24
    )
    arrived = lax.all_to_all(packed, "seq", 0, 0, tiled=True)
    rate_later, _ = lax.optimization_barrier((inner_rate, packed))
    given, made = [q, k, v, w, dz], [double, single, single]
    error, weights, gate, slope, source = call(
        trail_kernel,
        outside([rate_later] + given),
        inside([double, double]) + outside([apart(a) for a in made]),
        10 * unit,
        rate + buffers(given + made) + [flat, semaphores(5), semaphores(3)],
        LATE_LIMIT,
    )
    arrived, slope = lax.optimization_barrier((arrived, slope))
    (ends,) = call(
        partial(relay_kernel, group=8),
        inside([arrived]),
        inside([jax.ShapeDtypeStruct((shards, DH // 2 + 8, 128), BF16)]),
        unit,
        [pltpu.VMEM((shards, DH, 128), F32), pltpu.VMEM((shards, DH, 256), BF16)],
        24,
    )
    returned = lax.all_to_all(ends, "seq", 0, 0, tiled=True)
    rate_later, _ = lax.optimization_barrier((inner_rate, ends))
    grad_q, part = call(
        direct_kernel,
        outside([rate_later]) + inside([error, weights]) + outside([q, k, dz]),
        outside([whole, apart(single)]),
        10 * unit,
        rate + buffers([whole, whole, whole, whole, single]) + [semaphores(3), semaphores(2)],
        LATE_LIMIT,
    )
    held, made = [whole, double, single, single, single], [whole, whole, array(heads, F32, DH * DH)]
    grad_k, grad_v, start = call(
        final_kernel,
        outside([inner_rate]) + inside([returned, error, weights]) + outside([k, gate, slope, source, part]),
        outside(made),
        10 * unit,
        rate + buffers(held + made) + [flat, semaphores(5), semaphores(3)],
        LATE_LIMIT,
    )
    return grad_q[None], grad_k[None], grad_v[None], start[None, None]


def solution(mesh):
    tokens = P("section", "seq", None)
    return jax.shard_map(
        per_device,
        mesh=mesh,
        in_specs=(tokens, tokens, tokens, tokens, P("section", None), P("section", "seq", None, None)),
        out_specs=(tokens, tokens, tokens, P("section", "seq", None, None)),
        check_vma=False,
    )
```

```python
from functools import partial

import jax
import jax.numpy as jnp
from jax import lax
from jax.experimental import pallas as pl
from jax.experimental.pallas import tpu as pltpu
from jax.sharding import PartitionSpec as P

DH = 64
QUAD = 4 * DH
PAIRS = QUAD // 128
HEADS = QUAD // DH
F32 = jnp.float32
BF16 = jnp.bfloat16
JOINT = 2
CHUNKS = 4
MAP_LIMIT = 24
LATE_LIMIT = 24
CODE_SPAN = 250.0
CODE_BASE = -125.0


def quad_iota():
    row = lax.broadcasted_iota(jnp.int32, (DH, QUAD), 0)
    lane = lax.broadcasted_iota(jnp.int32, (DH, QUAD), 1)
    return row, lane % DH, lane // DH


def head_masks():
    head = quad_iota()[2]
    return [(head == h).astype(F32).astype(BF16) for h in range(QUAD // DH)]


def diagonal(right, masks):
    return jnp.concatenate([right * mask for mask in masks], axis=0)


def times(left, block):
    return lax.dot_general(left, block, (((1,), (0,)), ((), ())), preferred_element_type=F32)


def times_t(left, block):
    return lax.dot_general(left, block, (((1,), (1,)), ((), ())), preferred_element_type=F32)


def split(value):
    high = value.astype(BF16)
    low = (value - high.astype(F32)).astype(BF16)
    return high, low


def both(high, low):
    return jnp.concatenate([high, low], axis=0)


def folded(product):
    return product[:DH] + product[DH:]


def column_scale(value):
    largest = jnp.max(jnp.abs(value), axis=0, keepdims=True)
    return (jnp.maximum(largest, 1e-30) * 1.01).astype(BF16).astype(F32)


def encode(value, scale):
    size = jnp.exp2(jnp.abs(value) * (CODE_SPAN / scale) + CODE_BASE)
    return jnp.where(value < 0, -size, size)


def decode(code, scale):
    size = (jnp.log2(jnp.abs(code)) - CODE_BASE) * (scale / CODE_SPAN)
    return jnp.where(code < 0, -size, size)


def chunk(ref, i, features):
    if ref.shape[1] != features:
        size = ref.shape[0] // CHUNKS
        return ref.at[pl.ds(pl.multiple_of(i * size, size), size), :]
    size = features // CHUNKS
    return ref.at[:, pl.ds(pl.multiple_of(i * size, size), size)]


def rates(rate_ref, index):
    head = lax.broadcasted_iota(jnp.int32, (DH, QUAD), 1) // DH
    value = jnp.full((DH, QUAD), rate_ref[0, index * HEADS], F32)
    for h in range(1, HEADS):
        value = jnp.where(head == h, rate_ref[0, index * HEADS + h], value)
    return value * (1.0 / DH)


def mover(sources, targets, sems, features):
    def copies(i):
        return [
            pltpu.make_async_copy(chunk(source, i, features), chunk(target, i, features), sems.at[n, i])
            for n, (source, target) in enumerate(zip(sources, targets))
        ]

    def start(i):
        for copy in copies(i):
            copy.start()

    def wait(i):
        for copy in copies(i):
            copy.wait()

    return start, wait


def run(work, count, fetch, ship=None, first=None, joint=JOINT):
    each = count // CHUNKS
    first.start()
    for i in range(min(2 * joint, CHUNKS)):
        fetch[0](i)
    first.wait()

    def body(n, carry):
        for m in range(joint):
            i = n * joint + m
            fetch[1](i)

            @pl.when(i + 2 * joint < CHUNKS)
            def _():
                fetch[0](i + 2 * joint)

        for t in range(each * joint):
            index = n * each * joint + t
            work(index, pl.ds(pl.multiple_of(index * QUAD, QUAD), QUAD), t % each)
            if ship is not None and t % each == each - 1:
                ship[0](n * joint + t // each)
        return carry

    lax.fori_loop(0, CHUNKS // joint, body, 0)
    if ship is not None:
        for i in range(CHUNKS):
            ship[1](i)


def map_kernel(rate_hbm, q_hbm, k_hbm, acode_ref, ascale_ref, mt_ref, rate_ref, rate_sem, q_ref, k_ref, in_sems):
    row, col, _ = quad_iota()
    masks = head_masks()
    identity = (row == col).astype(F32).astype(BF16)
    upper = (row <= col).astype(F32)

    def work(index, lanes, t):
        rate = rates(rate_ref, index)
        gates, readouts = [], []
        for b in range(2):
            rows = slice(b * DH, (b + 1) * DH)
            k, q = k_ref[rows, lanes], q_ref[rows, lanes]
            k_block, q_block = diagonal(k, masks), diagonal(q, masks)
            on_q = times_t(both(k, identity), q_block)
            st_hi, st_lo = split(on_q[:DH] * upper)
            qt = on_q[DH:]
            kt = times_t(identity, k_block).astype(BF16)
            gates.append(rate * times(kt, k_block))
            readouts.append(qt - rate * (times(kt, diagonal(st_hi, masks)) + times(kt, diagonal(st_lo, masks))))
        g_hi, g_lo = split(gates[0])
        g_both = both(g_hi, g_lo)

        def gate_times(value):
            hi, lo = split(value)
            return folded(times(g_both, diagonal(hi, masks))) + times(g_hi, diagonal(lo, masks))

        drop = gates[0] + gates[1] - gate_times(gates[1])
        second = readouts[1] - gate_times(readouts[1])
        for b, value in enumerate((readouts[0], second)):
            hi, lo = split(value)
            mt_ref[b * 128 : b * 128 + 64, lanes] = hi
            mt_ref[b * 128 + 64 : b * 128 + 128, lanes] = lo
        scale = column_scale(drop)
        acode_ref[:, lanes] = encode(drop, scale).astype(BF16)
        ascale_ref[:, lanes] = jnp.broadcast_to(scale, (8, QUAD))

    features = k_ref.shape[1]
    fetch = mover((q_hbm, k_hbm), (q_ref, k_ref), in_sems, features)
    run(work, features // QUAD, fetch, None, pltpu.make_async_copy(rate_hbm, rate_ref, rate_sem))


def pack_kernel(mt_ref, dz_ref, acode_ref, ascale_ref, out_ref):
    masks = head_masks()
    left = lax.broadcasted_iota(jnp.int32, (DH, 128), 1) < DH
    left8 = left[:8]

    def work(index, lanes):
        total = folded(times(mt_ref[0:128, lanes], diagonal(dz_ref[0:DH, lanes], masks)))
        total += folded(times(mt_ref[128:256, lanes], diagonal(dz_ref[DH:128, lanes], masks)))
        scale = column_scale(total)
        code = encode(total, scale)
        a_code = acode_ref[:, lanes].astype(F32)
        a_scale = ascale_ref[:, lanes]
        scale = jnp.broadcast_to(scale, (8, QUAD))
        for p in range(PAIRS):
            cut = slice(p * 128, p * 128 + 128)
            head = index * HEADS + p * 2
            out_ref[head, 0:DH, :] = jnp.where(left, a_code[:, cut], pltpu.roll(code[:, cut], DH, 1)).astype(BF16)
            out_ref[head, DH : DH + 8, :] = jnp.where(left8, a_scale[:, cut], pltpu.roll(scale[:, cut], DH, 1)).astype(BF16)
            out_ref[head + 1, 0:DH, :] = jnp.where(left, pltpu.roll(a_code[:, cut], DH, 1), code[:, cut]).astype(BF16)
            out_ref[head + 1, DH : DH + 8, :] = jnp.where(left8, pltpu.roll(a_scale[:, cut], DH, 1), scale[:, cut]).astype(BF16)

    for index in range(dz_ref.shape[1] // QUAD):
        work(index, slice(index * QUAD, (index + 1) * QUAD))


def relay_kernel(in_ref, out_ref, map_ref, left_ref, group):
    shards = in_ref.shape[0]
    row = lax.broadcasted_iota(jnp.int32, (DH, 128), 0)
    lane = lax.broadcasted_iota(jnp.int32, (DH, 128), 1)
    left = lane < DH
    unit = (row == lane).astype(F32)

    def unpack(j):
        scale = in_ref[j, DH : DH + 8, :].astype(F32)[0:1]
        value = decode(in_ref[j, 0:DH, :].astype(F32), scale)
        return jnp.where(left, unit - value, value)

    def left_operand(value):
        hi, lo = split(value)
        hi_f = hi.astype(F32)
        lo_f = lo.astype(F32)
        first = jnp.where(left, hi_f, pltpu.roll(lo_f, DH, 1)).astype(BF16)
        last = jnp.where(left, hi_f, 0.0).astype(BF16)
        return jnp.concatenate([first, last], axis=1)

    def right_operand(value):
        hi, lo = split(value)
        return jnp.concatenate([hi, hi, lo, jnp.zeros_like(lo)], axis=0)

    def compose(own, behind):
        return times(left_operand(own), right_operand(behind)) + jnp.where(left, 0.0, own)

    def apply(own, end):
        return times(left_operand(own), right_operand(end)) + own

    groups = shards // group
    suffix = []
    for g in range(groups):
        j = g * group + group - 1
        suffix.append(unpack(j))
        map_ref[j] = suffix[g]
        left_ref[j] = left_operand(suffix[g])
    for step in range(group - 2, -1, -1):
        for g in range(groups):
            j = g * group + step
            suffix[g] = compose(unpack(j), suffix[g])
            map_ref[j] = suffix[g]
            left_ref[j] = left_operand(suffix[g])
    runs = groups // group
    for step in range(group - 2, -1, -1):
        for u in range(runs):
            g = u * group + step
            suffix[g] = compose(suffix[g], suffix[g + 1])
    ends = [None] * groups
    end = None
    for u in range(runs - 1, -1, -1):
        first, last = u * group, u * group + group - 1
        for g in range(first, last):
            ends[g] = suffix[g + 1] if end is None else apply(suffix[g + 1], end)
        ends[last] = jnp.zeros((DH, 128), F32) if end is None else end
        end = suffix[first] if end is None else apply(suffix[first], end)
    for g in range(groups):
        right = right_operand(ends[g])
        found = []
        for step in range(group):
            j = g * group + step
            if step == group - 1:
                found.append(ends[g])
            else:
                found.append(times(left_ref[j + 1], right) + map_ref[j + 1])
        for step in range(0, group, 2):
            pair = jnp.where(left, pltpu.roll(found[step], DH, 1), found[step + 1])
            scale = column_scale(pair)
            code = encode(pair, scale)
            turned = pltpu.roll(code, DH, 1)
            scale = jnp.broadcast_to(scale, (8, 128))
            j = g * group + step
            half = DH // 2
            low = left[:half]
            out_ref[j, 0:half, :] = jnp.where(low, code[:half], turned[half:]).astype(BF16)
            other = pltpu.roll(scale, DH, 1)
            out_ref[j, half : half + 8, :] = jnp.where(left[:8], scale, other).astype(BF16)
            out_ref[j + 1, 0:half, :] = jnp.where(low, turned[:half], code[half:]).astype(BF16)
            out_ref[j + 1, half : half + 8, :] = jnp.where(left[:8], other, scale).astype(BF16)


def trail_kernel(rate_hbm, *refs):
    inputs, e_ref, outputs, (rate_ref, rate_sem) = refs[:5], refs[5], refs[6:10], refs[10:12]
    q_ref, k_ref, v_ref, w_ref, dz_ref = refs[12:17]
    weight_ref, gate_ref, t_ref, source_ref = refs[17:21]
    flat_ref, in_sems, out_sems = refs[21:]
    row, col, _ = quad_iota()
    masks = head_masks()
    identity = (row == col).astype(F32).astype(BF16)
    upper = (row <= col).astype(F32)
    half = DH // 2
    low = lax.broadcasted_iota(jnp.int32, (half, 128), 1) < DH

    def start_weight(pair):
        first = pl.multiple_of(pair * DH, DH)
        one = flat_ref[pl.ds(first, half), :]
        two = flat_ref[pl.ds(first + half, half), :]
        even = jnp.where(low, one, pltpu.roll(two, DH, 1))
        odd = jnp.where(low, pltpu.roll(one, DH, 1), two)
        flat_ref[pl.ds(first, half, stride=2), :] = even
        flat_ref[pl.ds(first + 1, half, stride=2), :] = odd
        return flat_ref[pl.ds(first, DH), :]

    def work(index, lanes, t):
        rate = rates(rate_ref, index)
        if t == 0:
            first = pl.multiple_of(index * HEADS, 8)
            for i in range(half):
                flat_ref[pl.ds(first * half + i, 8, stride=half), :] = w_ref[pl.ds(first, 8), i * 128 : (i + 1) * 128]
        weight = jnp.concatenate([start_weight(index * PAIRS + p) for p in range(PAIRS)], axis=1)
        for b in range(2):
            rows = slice(b * DH, (b + 1) * DH)
            hi_rows, lo_rows = slice(b * 128, b * 128 + 64), slice(b * 128 + 64, b * 128 + 128)
            k = k_ref[rows, lanes]
            w_hi, w_lo = split(weight)
            w_block, w_low_block = diagonal(w_hi, masks), diagonal(w_lo, masks)
            weight_ref[hi_rows, lanes] = w_hi
            weight_ref[lo_rows, lanes] = w_lo
            error = times(k, w_block) + times(k, w_low_block) - v_ref[rows, lanes].astype(F32)
            e_hi, e_lo = split(error)
            e_ref[hi_rows, lanes] = e_hi
            e_ref[lo_rows, lanes] = e_lo
            k_block = diagonal(k, masks)
            kt = times_t(identity, k_block).astype(BF16)
            gate_hi, gate_lo = split(rate * times(kt, k_block))
            gate_ref[hi_rows, lanes] = gate_hi
            gate_ref[lo_rows, lanes] = gate_lo
            if b == 0:
                weight = weight - rate * (times(kt, diagonal(e_hi, masks)) + times(kt, diagonal(e_lo, masks)))
            on_q = times_t(both(k, identity), diagonal(q_ref[rows, lanes], masks))
            st_hi, st_lo = split(on_q[:DH] * upper)
            qt = on_q[DH:].astype(BF16)
            on_dz = times(jnp.concatenate([st_hi, st_lo, qt], axis=0), diagonal(dz_ref[rows, lanes], masks))
            slope = on_dz[:DH] + on_dz[DH:128]
            t_ref[rows, lanes] = slope
            t_hi, t_lo = split(slope)
            source_ref[rows, lanes] = on_dz[128:] - rate * (times(kt, diagonal(t_hi, masks)) + times(kt, diagonal(t_lo, masks)))

    features = k_ref.shape[1]
    fetch = mover(inputs, refs[12:17], in_sems, features)
    ship = mover(refs[17:21], outputs, out_sems, features)
    run(work, features // QUAD, fetch, ship, pltpu.make_async_copy(rate_hbm, rate_ref, rate_sem))


def direct_kernel(rate_hbm, e_ref, *refs):
    inputs, outputs, wt_ref, (rate_ref, rate_sem) = refs[:4], refs[4:6], refs[6], refs[7:9]
    q_ref, k_ref, dz_ref, weight_ref, gq_ref, part_ref, in_sems, out_sems = refs[9:]
    row, col, _ = quad_iota()
    masks = head_masks()
    identity = (row == col).astype(F32).astype(BF16)
    upper = (row <= col).astype(F32)
    lower = (row >= col).astype(F32)

    def work(index, lanes, t):
        rate = rates(rate_ref, index)
        for b in range(2):
            rows = slice(b * DH, (b + 1) * DH)
            two = slice(b * 128, b * 128 + 128)
            hi_rows, lo_rows = slice(b * 128, b * 128 + 64), slice(b * 128 + 64, b * 128 + 128)
            dz = dz_ref[rows, lanes]
            dpt = folded(times_t(e_ref[two, lanes], diagonal(dz, masks))) * (-rate * upper)
            dp = times_t(dz, diagonal(e_ref[hi_rows, lanes], masks)) + times_t(dz, diagonal(e_ref[lo_rows, lanes], masks))
            dp = dp * (-rate * lower)
            left = both(dz, identity)
            high = times_t(left, diagonal(weight_ref[hi_rows, lanes], masks))
            low = times_t(left, diagonal(weight_ref[lo_rows, lanes], masks))
            wt_ref[hi_rows, lanes] = high[DH:].astype(BF16)
            wt_ref[lo_rows, lanes] = low[DH:].astype(BF16)
            grad = high[:DH] + low[:DH]
            grad += folded(times(both(*split(dp)), diagonal(k_ref[rows, lanes], masks)))
            gq_ref[rows, lanes] = grad.astype(BF16)
            part_ref[rows, lanes] = folded(times(both(*split(dpt)), diagonal(q_ref[rows, lanes], masks)))

    features = k_ref.shape[1]
    fetch = mover(inputs, (q_ref, k_ref, dz_ref, weight_ref), in_sems, features)
    ship = mover((gq_ref, part_ref), outputs, out_sems, features)
    run(work, features // QUAD, fetch, ship, pltpu.make_async_copy(rate_hbm, rate_ref, rate_sem))


def final_kernel(rate_hbm, code_ref, e_ref, wt_ref, *refs):
    inputs, outputs, (rate_ref, rate_sem) = refs[:5], refs[5:8], refs[8:10]
    k_ref, gate_ref, t_ref, source_ref, part_ref = refs[10:15]
    gk_ref, gv_ref, start_ref, flat_ref, in_sems, out_sems = refs[15:]
    masks = head_masks()
    half = DH // 2
    low = lax.broadcasted_iota(jnp.int32, (half, 128), 1) < DH

    def work(index, lanes, t):
        rate = rates(rate_ref, index)
        pairs = []
        for p in range(PAIRS):
            halves = []
            for h in range(2):
                head = index * HEADS + p * 2 + h
                scale = code_ref[head, half : half + 8, :].astype(F32)[0:1]
                halves.append(decode(code_ref[head, 0:half, :].astype(F32), scale))
            top = jnp.where(low, halves[0], pltpu.roll(halves[1], DH, 1))
            bottom = jnp.where(low, pltpu.roll(halves[0], DH, 1), halves[1])
            pairs.append(jnp.concatenate([top, bottom], axis=0))
        adjoint = jnp.concatenate(pairs, axis=1)
        for b in (1, 0):
            rows = slice(b * DH, (b + 1) * DH)
            two = slice(b * 128, b * 128 + 128)
            hi_rows, lo_rows = slice(b * 128, b * 128 + 64), slice(b * 128 + 64, b * 128 + 128)
            g_hi, g_lo = split(adjoint)
            g_block, g_low_block = diagonal(g_hi, masks), diagonal(g_lo, masks)
            k, gate = k_ref[rows, lanes], gate_ref[two, lanes]
            high = times(jnp.concatenate([k, gate], axis=0), g_block)
            low_part = times(jnp.concatenate([k, gate[:DH]], axis=0), g_low_block)
            slope = t_ref[rows, lanes] + high[:DH] + low_part[:DH]
            adjoint = adjoint - (folded(high[DH:]) + low_part[DH:]) + source_ref[rows, lanes]
            grad_error = -rate * slope
            gv_ref[rows, lanes] = (-grad_error).astype(BF16)
            d_hi, d_lo = split(grad_error)
            grad = part_ref[rows, lanes]
            grad += folded(times(both(d_hi, d_lo), diagonal(wt_ref[hi_rows, lanes], masks)))
            grad += times(d_hi, diagonal(wt_ref[lo_rows, lanes], masks))
            on_g = folded(times_t(e_ref[two, lanes], g_block)) + times_t(e_ref[hi_rows, lanes], g_low_block)
            gk_ref[rows, lanes] = (grad - rate * on_g).astype(BF16)
        for p in range(PAIRS):
            first = pl.multiple_of((index * PAIRS + p) * DH, DH)
            flat_ref[pl.ds(first, DH), :] = adjoint[:, p * 128 : p * 128 + 128]
            even = flat_ref[pl.ds(first, half, stride=2), :]
            odd = flat_ref[pl.ds(first + 1, half, stride=2), :]
            flat_ref[pl.ds(first, half), :] = jnp.where(low, even, pltpu.roll(odd, DH, 1))
            flat_ref[pl.ds(first + half, half), :] = jnp.where(low, pltpu.roll(even, DH, 1), odd)
        if (t + 1) * HEADS == 8:
            head = pl.multiple_of((index + 1) * HEADS - 8, 8)
            for i in range(half):
                start_ref[pl.ds(head, 8), i * 128 : (i + 1) * 128] = flat_ref[pl.ds(head * half + i, 8, stride=half), :]

    features = k_ref.shape[1]
    fetch = mover(inputs, refs[10:15], in_sems, features)
    ship = mover((gk_ref, gv_ref, start_ref), outputs, out_sems, features)
    run(work, features // QUAD, fetch, ship, pltpu.make_async_copy(rate_hbm, rate_ref, rate_sem))


def call(kernel, ins, outs, flops, scratch=(), limit=58):
    args = [array for array, _ in ins]
    size = sum(a.size * a.dtype.itemsize for a in args) + sum(o.size * o.dtype.itemsize for o, _ in outs)
    return pl.pallas_call(
        kernel,
        out_shape=tuple(shape if memory is pltpu.VMEM else pltpu.HBM(shape.shape, shape.dtype) for shape, memory in outs),
        in_specs=[pl.BlockSpec(memory_space=memory) for _, memory in ins],
        out_specs=tuple(pl.BlockSpec(memory_space=memory) for _, memory in outs),
        scratch_shapes=list(scratch),
        compiler_params=pltpu.CompilerParams(vmem_limit_bytes=limit * 1024 * 1024),
        cost_estimate=pl.CostEstimate(flops=flops, bytes_accessed=size, transcendentals=0),
    )(*args)


def per_device(queries, memory_keys, memory_values, upstream, inner_rate, checkpoints):
    sections = lax.axis_size("section")
    shards = lax.axis_size("seq")
    heads = inner_rate.shape[1]
    features = queries.shape[2]
    tokens = queries.shape[1]
    q, k, v, w = queries[0], memory_keys[0], memory_values[0], checkpoints[0, 0]

    def array(rows, kind, columns=features):
        return jax.ShapeDtypeStruct((rows, columns), kind)

    def apart(a):
        return jax.ShapeDtypeStruct((a.shape[0] * CHUNKS, a.shape[1] // CHUNKS), a.dtype)

    def buffers(arrays):
        return [pltpu.VMEM(a.shape, a.dtype) for a in arrays]

    def semaphores(count):
        return pltpu.SemaphoreType.DMA((count, CHUNKS))

    def outside(arrays):
        return [(a if isinstance(a, jax.ShapeDtypeStruct) else pltpu.with_memory_space_constraint(a, pltpu.HBM), pltpu.HBM) for a in arrays]

    def inside(arrays):
        return [(a, pltpu.VMEM) for a in arrays]

    unit = 2 * tokens * features * QUAD
    flat = pltpu.VMEM((heads * DH // 2, 128), F32)
    single, whole, double = array(tokens, F32), array(tokens, BF16), array(2 * tokens, BF16)
    rate = [pltpu.SMEM(inner_rate.shape, F32), pltpu.SemaphoreType.DMA]

    cotangent = lax.ppermute(upstream, "section", [((i + 1) % sections, i) for i in range(sections)])
    dz = cotangent[0]
    acode, ascale, mt = call(
        map_kernel,
        outside([inner_rate, q, k]),
        inside([array(DH, BF16), array(8, F32), double]),
        8 * unit,
        rate + buffers([q, k]) + [semaphores(2)],
        MAP_LIMIT,
    )
    (packed,) = call(
        pack_kernel, inside([mt, dz, acode, ascale]), inside([jax.ShapeDtypeStruct((heads, DH + 8, 128), BF16)]), 2 * unit, (), 24
    )
    arrived = lax.all_to_all(packed, "seq", 0, 0, tiled=True)
    rate_later, _ = lax.optimization_barrier((inner_rate, packed))
    given, made = [q, k, v, w, dz], [double, double, single, single]
    error, weights, gate, slope, source = call(
        trail_kernel,
        outside([rate_later] + given),
        inside([double]) + outside([apart(a) for a in made]),
        10 * unit,
        rate + buffers(given + made) + [flat, semaphores(5), semaphores(4)],
        LATE_LIMIT,
    )
    arrived, slope = lax.optimization_barrier((arrived, slope))
    (ends,) = call(
        partial(relay_kernel, group=4),
        inside([arrived]),
        inside([jax.ShapeDtypeStruct((shards, DH // 2 + 8, 128), BF16)]),
        unit,
        [pltpu.VMEM((shards, DH, 128), F32), pltpu.VMEM((shards, DH, 256), BF16)],
        24,
    )
    returned = lax.all_to_all(ends, "seq", 0, 0, tiled=True)
    rate_later, _ = lax.optimization_barrier((inner_rate, ends))
    grad_q, part, turned = call(
        direct_kernel,
        outside([rate_later]) + inside([error]) + outside([q, k, dz, weights]),
        outside([whole, apart(single)]) + inside([double]),
        10 * unit,
        rate + buffers([whole, whole, whole, double, whole, single]) + [semaphores(4), semaphores(2)],
        LATE_LIMIT,
    )
    held, made = [whole, double, single, single, single], [whole, whole, array(heads, F32, DH * DH)]
    grad_k, grad_v, start = call(
        final_kernel,
        outside([inner_rate]) + inside([returned, error, turned]) + outside([k, gate, slope, source, part]),
        outside(made),
        10 * unit,
        rate + buffers(held + made) + [flat, semaphores(5), semaphores(3)],
        LATE_LIMIT,
    )
    return grad_q[None], grad_k[None], grad_v[None], start[None, None]


def solution(mesh):
    tokens = P("section", "seq", None)
    return jax.shard_map(
        per_device,
        mesh=mesh,
        in_specs=(tokens, tokens, tokens, tokens, P("section", None), P("section", "seq", None, None)),
        out_specs=(tokens, tokens, tokens, P("section", "seq", None, None)),
        check_vma=False,
    )
```

```python
from functools import partial

import jax
import jax.numpy as jnp
from jax import lax
from jax.experimental import pallas as pl
from jax.experimental.pallas import tpu as pltpu
from jax.sharding import PartitionSpec as P

DH = 64
QUAD = 4 * DH
PAIRS = QUAD // 128
HEADS = QUAD // DH
F32 = jnp.float32
BF16 = jnp.bfloat16
JOINT = 2
CHUNKS = 4
MAP_LIMIT = 24
LATE_LIMIT = 24
CODE_SPAN = 250.0
CODE_BASE = -125.0


def quad_iota():
    row = lax.broadcasted_iota(jnp.int32, (DH, QUAD), 0)
    lane = lax.broadcasted_iota(jnp.int32, (DH, QUAD), 1)
    return row, lane % DH, lane // DH


def head_masks():
    head = quad_iota()[2]
    return [(head == h).astype(F32).astype(BF16) for h in range(QUAD // DH)]


def diagonal(right, masks):
    return jnp.concatenate([right * mask for mask in masks], axis=0)


def times(left, block):
    return lax.dot_general(left, block, (((1,), (0,)), ((), ())), preferred_element_type=F32)


def times_t(left, block):
    return lax.dot_general(left, block, (((1,), (1,)), ((), ())), preferred_element_type=F32)


def split(value):
    high = value.astype(BF16)
    low = (value - high.astype(F32)).astype(BF16)
    return high, low


def both(high, low):
    return jnp.concatenate([high, low], axis=0)


def folded(product):
    return product[:DH] + product[DH:]


def column_scale(value):
    largest = jnp.max(jnp.abs(value), axis=0, keepdims=True)
    return (jnp.maximum(largest, 1e-30) * 1.01).astype(BF16).astype(F32)


def encode(value, scale):
    size = jnp.exp2(jnp.abs(value) * (CODE_SPAN / scale) + CODE_BASE)
    return jnp.where(value < 0, -size, size)


def decode(code, scale):
    size = (jnp.log2(jnp.abs(code)) - CODE_BASE) * (scale / CODE_SPAN)
    return jnp.where(code < 0, -size, size)


def chunk(ref, i, features):
    if ref.shape[1] != features:
        size = ref.shape[0] // CHUNKS
        return ref.at[pl.ds(pl.multiple_of(i * size, size), size), :]
    size = features // CHUNKS
    return ref.at[:, pl.ds(pl.multiple_of(i * size, size), size)]


def rates(rate_ref, index):
    head = lax.broadcasted_iota(jnp.int32, (DH, QUAD), 1) // DH
    value = jnp.full((DH, QUAD), rate_ref[0, index * HEADS], F32)
    for h in range(1, HEADS):
        value = jnp.where(head == h, rate_ref[0, index * HEADS + h], value)
    return value * (1.0 / DH)


def mover(sources, targets, sems, features):
    def copies(i):
        return [
            pltpu.make_async_copy(chunk(source, i, features), chunk(target, i, features), sems.at[n, i])
            for n, (source, target) in enumerate(zip(sources, targets))
        ]

    def start(i):
        for copy in copies(i):
            copy.start()

    def wait(i):
        for copy in copies(i):
            copy.wait()

    return start, wait


def run(work, count, fetch, ship=None, first=None, joint=JOINT):
    each = count // CHUNKS
    first.start()
    for i in range(min(2 * joint, CHUNKS)):
        fetch[0](i)
    first.wait()

    def body(n, carry):
        for m in range(joint):
            i = n * joint + m
            fetch[1](i)

            @pl.when(i + 2 * joint < CHUNKS)
            def _():
                fetch[0](i + 2 * joint)

        for t in range(each * joint):
            index = n * each * joint + t
            work(index, pl.ds(pl.multiple_of(index * QUAD, QUAD), QUAD), t % each)
            if ship is not None and t % each == each - 1:
                ship[0](n * joint + t // each)
        return carry

    lax.fori_loop(0, CHUNKS // joint, body, 0)
    if ship is not None:
        for i in range(CHUNKS):
            ship[1](i)


def part_copy(source, target, sems, i):
    size = source.shape[0] // CHUNKS
    return pltpu.make_async_copy(source.at[pl.ds(i * size, size)], target.at[pl.ds(i * size, size)], sems.at[i])


def map_kernel(rate_hbm, q_hbm, k_hbm, acode_ref, ascale_ref, mt_ref, rate_ref, rate_sem, q_ref, k_ref, in_sems):
    row, col, _ = quad_iota()
    masks = head_masks()
    identity = (row == col).astype(F32).astype(BF16)
    upper = (row <= col).astype(F32)

    def work(index, lanes, t):
        rate = rates(rate_ref, index)
        gates, readouts = [], []
        for b in range(2):
            rows = slice(b * DH, (b + 1) * DH)
            k, q = k_ref[rows, lanes], q_ref[rows, lanes]
            k_block, q_block = diagonal(k, masks), diagonal(q, masks)
            on_q = times_t(both(k, identity), q_block)
            st_hi, st_lo = split(on_q[:DH] * upper)
            qt = on_q[DH:]
            kt = times_t(identity, k_block).astype(BF16)
            gates.append(rate * times(kt, k_block))
            readouts.append(qt - rate * (times(kt, diagonal(st_hi, masks)) + times(kt, diagonal(st_lo, masks))))
        g_hi, g_lo = split(gates[0])
        g_both = both(g_hi, g_lo)

        def gate_times(value):
            hi, lo = split(value)
            return folded(times(g_both, diagonal(hi, masks))) + times(g_hi, diagonal(lo, masks))

        drop = gates[0] + gates[1] - gate_times(gates[1])
        second = readouts[1] - gate_times(readouts[1])
        for b, value in enumerate((readouts[0], second)):
            hi, lo = split(value)
            mt_ref[b * 128 : b * 128 + 64, lanes] = hi
            mt_ref[b * 128 + 64 : b * 128 + 128, lanes] = lo
        scale = column_scale(drop)
        acode_ref[:, lanes] = encode(drop, scale).astype(BF16)
        ascale_ref[:, lanes] = jnp.broadcast_to(scale, (8, QUAD))

    features = k_ref.shape[1]
    fetch = mover((q_hbm, k_hbm), (q_ref, k_ref), in_sems, features)
    run(work, features // QUAD, fetch, None, pltpu.make_async_copy(rate_hbm, rate_ref, rate_sem))


def pack_kernel(mt_ref, dz_ref, acode_ref, ascale_ref, out_hbm, out_ref, sems):
    masks = head_masks()
    left = lax.broadcasted_iota(jnp.int32, (DH, 128), 1) < DH
    left8 = left[:8]

    def work(index, lanes):
        total = folded(times(mt_ref[0:128, lanes], diagonal(dz_ref[0:DH, lanes], masks)))
        total += folded(times(mt_ref[128:256, lanes], diagonal(dz_ref[DH:128, lanes], masks)))
        scale = column_scale(total)
        code = encode(total, scale)
        a_code = acode_ref[:, lanes].astype(F32)
        a_scale = ascale_ref[:, lanes]
        scale = jnp.broadcast_to(scale, (8, QUAD))
        for p in range(PAIRS):
            cut = slice(p * 128, p * 128 + 128)
            head = index * HEADS + p * 2
            out_ref[head, 0:DH, :] = jnp.where(left, a_code[:, cut], pltpu.roll(code[:, cut], DH, 1)).astype(BF16)
            out_ref[head, DH : DH + 8, :] = jnp.where(left8, a_scale[:, cut], pltpu.roll(scale[:, cut], DH, 1)).astype(BF16)
            out_ref[head + 1, 0:DH, :] = jnp.where(left, pltpu.roll(a_code[:, cut], DH, 1), code[:, cut]).astype(BF16)
            out_ref[head + 1, DH : DH + 8, :] = jnp.where(left8, pltpu.roll(a_scale[:, cut], DH, 1), scale[:, cut]).astype(BF16)

    each = dz_ref.shape[1] // QUAD // CHUNKS
    for index in range(each * CHUNKS):
        work(index, slice(index * QUAD, (index + 1) * QUAD))
        if index % each == each - 1:
            part_copy(out_ref, out_hbm, sems, index // each).start()
    for i in range(CHUNKS):
        part_copy(out_ref, out_hbm, sems, i).wait()


def relay_kernel(in_ref, out_hbm, out_ref, map_ref, left_ref, sems, group):
    shards = in_ref.shape[0]
    row = lax.broadcasted_iota(jnp.int32, (DH, 128), 0)
    lane = lax.broadcasted_iota(jnp.int32, (DH, 128), 1)
    left = lane < DH
    unit = (row == lane).astype(F32)

    def unpack(j):
        scale = in_ref[j, DH : DH + 8, :].astype(F32)[0:1]
        value = decode(in_ref[j, 0:DH, :].astype(F32), scale)
        return jnp.where(left, unit - value, value)

    def left_operand(value):
        hi, lo = split(value)
        hi_f = hi.astype(F32)
        lo_f = lo.astype(F32)
        first = jnp.where(left, hi_f, pltpu.roll(lo_f, DH, 1)).astype(BF16)
        last = jnp.where(left, hi_f, 0.0).astype(BF16)
        return jnp.concatenate([first, last], axis=1)

    def right_operand(value):
        hi, lo = split(value)
        return jnp.concatenate([hi, hi, lo, jnp.zeros_like(lo)], axis=0)

    def compose(own, behind):
        return times(left_operand(own), right_operand(behind)) + jnp.where(left, 0.0, own)

    def apply(own, end):
        return times(left_operand(own), right_operand(end)) + own

    groups = shards // group
    suffix = []
    for g in range(groups):
        j = g * group + group - 1
        suffix.append(unpack(j))
        map_ref[j] = suffix[g]
        left_ref[j] = left_operand(suffix[g])
    for step in range(group - 2, -1, -1):
        for g in range(groups):
            j = g * group + step
            suffix[g] = compose(unpack(j), suffix[g])
            map_ref[j] = suffix[g]
            left_ref[j] = left_operand(suffix[g])
    runs = groups // group
    for step in range(group - 2, -1, -1):
        for u in range(runs):
            g = u * group + step
            suffix[g] = compose(suffix[g], suffix[g + 1])
    ends = [None] * groups
    end = None
    for u in range(runs - 1, -1, -1):
        first, last = u * group, u * group + group - 1
        for g in range(first, last):
            ends[g] = suffix[g + 1] if end is None else apply(suffix[g + 1], end)
        ends[last] = jnp.zeros((DH, 128), F32) if end is None else end
        end = suffix[first] if end is None else apply(suffix[first], end)
    for g in range(groups):
        right = right_operand(ends[g])
        found = []
        for step in range(group):
            j = g * group + step
            if step == group - 1:
                found.append(ends[g])
            else:
                found.append(times(left_ref[j + 1], right) + map_ref[j + 1])
        for step in range(0, group, 2):
            pair = jnp.where(left, pltpu.roll(found[step], DH, 1), found[step + 1])
            scale = column_scale(pair)
            code = encode(pair, scale)
            turned = pltpu.roll(code, DH, 1)
            scale = jnp.broadcast_to(scale, (8, 128))
            j = g * group + step
            half = DH // 2
            low = left[:half]
            out_ref[j, 0:half, :] = jnp.where(low, code[:half], turned[half:]).astype(BF16)
            other = pltpu.roll(scale, DH, 1)
            out_ref[j, half : half + 8, :] = jnp.where(left[:8], scale, other).astype(BF16)
            out_ref[j + 1, 0:half, :] = jnp.where(low, turned[:half], code[half:]).astype(BF16)
            out_ref[j + 1, half : half + 8, :] = jnp.where(left[:8], other, scale).astype(BF16)
        size = shards // CHUNKS
        if (g + 1) * group % size == 0:
            part_copy(out_ref, out_hbm, sems, ((g + 1) * group - 1) // size).start()
    for i in range(CHUNKS):
        part_copy(out_ref, out_hbm, sems, i).wait()


def trail_kernel(rate_hbm, *refs):
    inputs, e_ref, outputs, (rate_ref, rate_sem) = refs[:5], refs[5], refs[6:10], refs[10:12]
    q_ref, k_ref, v_ref, w_ref, dz_ref = refs[12:17]
    weight_ref, gate_ref, t_ref, source_ref = refs[17:21]
    flat_ref, in_sems, out_sems = refs[21:]
    row, col, _ = quad_iota()
    masks = head_masks()
    identity = (row == col).astype(F32).astype(BF16)
    upper = (row <= col).astype(F32)
    half = DH // 2
    low = lax.broadcasted_iota(jnp.int32, (half, 128), 1) < DH

    def start_weight(pair):
        first = pl.multiple_of(pair * DH, DH)
        one = flat_ref[pl.ds(first, half), :]
        two = flat_ref[pl.ds(first + half, half), :]
        even = jnp.where(low, one, pltpu.roll(two, DH, 1))
        odd = jnp.where(low, pltpu.roll(one, DH, 1), two)
        flat_ref[pl.ds(first, half, stride=2), :] = even
        flat_ref[pl.ds(first + 1, half, stride=2), :] = odd
        return flat_ref[pl.ds(first, DH), :]

    def work(index, lanes, t):
        rate = rates(rate_ref, index)
        if t == 0:
            first = pl.multiple_of(index * HEADS, 8)
            for i in range(half):
                flat_ref[pl.ds(first * half + i, 8, stride=half), :] = w_ref[pl.ds(first, 8), i * 128 : (i + 1) * 128]
        weight = jnp.concatenate([start_weight(index * PAIRS + p) for p in range(PAIRS)], axis=1)
        for b in range(2):
            rows = slice(b * DH, (b + 1) * DH)
            hi_rows, lo_rows = slice(b * 128, b * 128 + 64), slice(b * 128 + 64, b * 128 + 128)
            k = k_ref[rows, lanes]
            w_hi, w_lo = split(weight)
            w_block, w_low_block = diagonal(w_hi, masks), diagonal(w_lo, masks)
            weight_ref[hi_rows, lanes] = w_hi
            weight_ref[lo_rows, lanes] = w_lo
            error = times(k, w_block) + times(k, w_low_block) - v_ref[rows, lanes].astype(F32)
            e_hi, e_lo = split(error)
            e_ref[hi_rows, lanes] = e_hi
            e_ref[lo_rows, lanes] = e_lo
            k_block = diagonal(k, masks)
            kt = times_t(identity, k_block).astype(BF16)
            gate_hi, gate_lo = split(rate * times(kt, k_block))
            gate_ref[hi_rows, lanes] = gate_hi
            gate_ref[lo_rows, lanes] = gate_lo
            if b == 0:
                weight = weight - rate * (times(kt, diagonal(e_hi, masks)) + times(kt, diagonal(e_lo, masks)))
            on_q = times_t(both(k, identity), diagonal(q_ref[rows, lanes], masks))
            st_hi, st_lo = split(on_q[:DH] * upper)
            qt = on_q[DH:].astype(BF16)
            on_dz = times(jnp.concatenate([st_hi, st_lo, qt], axis=0), diagonal(dz_ref[rows, lanes], masks))
            slope = on_dz[:DH] + on_dz[DH:128]
            t_ref[rows, lanes] = slope
            t_hi, t_lo = split(slope)
            source_ref[rows, lanes] = on_dz[128:] - rate * (times(kt, diagonal(t_hi, masks)) + times(kt, diagonal(t_lo, masks)))

    features = k_ref.shape[1]
    fetch = mover(inputs, refs[12:17], in_sems, features)
    ship = mover(refs[17:21], outputs, out_sems, features)
    run(work, features // QUAD, fetch, ship, pltpu.make_async_copy(rate_hbm, rate_ref, rate_sem))


def direct_kernel(rate_hbm, e_ref, *refs):
    inputs, outputs, wt_ref, (rate_ref, rate_sem) = refs[:4], refs[4:6], refs[6], refs[7:9]
    q_ref, k_ref, dz_ref, weight_ref, gq_ref, part_ref, in_sems, out_sems = refs[9:]
    row, col, _ = quad_iota()
    masks = head_masks()
    identity = (row == col).astype(F32).astype(BF16)
    upper = (row <= col).astype(F32)
    lower = (row >= col).astype(F32)

    def work(index, lanes, t):
        rate = rates(rate_ref, index)
        for b in range(2):
            rows = slice(b * DH, (b + 1) * DH)
            two = slice(b * 128, b * 128 + 128)
            hi_rows, lo_rows = slice(b * 128, b * 128 + 64), slice(b * 128 + 64, b * 128 + 128)
            dz = dz_ref[rows, lanes]
            dpt = folded(times_t(e_ref[two, lanes], diagonal(dz, masks))) * (-rate * upper)
            dp = times_t(dz, diagonal(e_ref[hi_rows, lanes], masks)) + times_t(dz, diagonal(e_ref[lo_rows, lanes], masks))
            dp = dp * (-rate * lower)
            left = both(dz, identity)
            high = times_t(left, diagonal(weight_ref[hi_rows, lanes], masks))
            low = times_t(left, diagonal(weight_ref[lo_rows, lanes], masks))
            wt_ref[hi_rows, lanes] = high[DH:].astype(BF16)
            wt_ref[lo_rows, lanes] = low[DH:].astype(BF16)
            grad = high[:DH] + low[:DH]
            grad += folded(times(both(*split(dp)), diagonal(k_ref[rows, lanes], masks)))
            gq_ref[rows, lanes] = grad.astype(BF16)
            part_ref[rows, lanes] = folded(times(both(*split(dpt)), diagonal(q_ref[rows, lanes], masks)))

    features = k_ref.shape[1]
    fetch = mover(inputs, (q_ref, k_ref, dz_ref, weight_ref), in_sems, features)
    ship = mover((gq_ref, part_ref), outputs, out_sems, features)
    run(work, features // QUAD, fetch, ship, pltpu.make_async_copy(rate_hbm, rate_ref, rate_sem))


def final_kernel(rate_hbm, code_ref, e_ref, wt_ref, *refs):
    inputs, outputs, (rate_ref, rate_sem) = refs[:5], refs[5:8], refs[8:10]
    k_ref, gate_ref, t_ref, source_ref, part_ref = refs[10:15]
    gk_ref, gv_ref, start_ref, flat_ref, in_sems, out_sems = refs[15:]
    masks = head_masks()
    half = DH // 2
    low = lax.broadcasted_iota(jnp.int32, (half, 128), 1) < DH

    def work(index, lanes, t):
        rate = rates(rate_ref, index)
        pairs = []
        for p in range(PAIRS):
            halves = []
            for h in range(2):
                head = index * HEADS + p * 2 + h
                scale = code_ref[head, half : half + 8, :].astype(F32)[0:1]
                halves.append(decode(code_ref[head, 0:half, :].astype(F32), scale))
            top = jnp.where(low, halves[0], pltpu.roll(halves[1], DH, 1))
            bottom = jnp.where(low, pltpu.roll(halves[0], DH, 1), halves[1])
            pairs.append(jnp.concatenate([top, bottom], axis=0))
        adjoint = jnp.concatenate(pairs, axis=1)
        for b in (1, 0):
            rows = slice(b * DH, (b + 1) * DH)
            two = slice(b * 128, b * 128 + 128)
            hi_rows, lo_rows = slice(b * 128, b * 128 + 64), slice(b * 128 + 64, b * 128 + 128)
            g_hi, g_lo = split(adjoint)
            g_block, g_low_block = diagonal(g_hi, masks), diagonal(g_lo, masks)
            k, gate = k_ref[rows, lanes], gate_ref[two, lanes]
            high = times(jnp.concatenate([k, gate], axis=0), g_block)
            low_part = times(jnp.concatenate([k, gate[:DH]], axis=0), g_low_block)
            slope = t_ref[rows, lanes] + high[:DH] + low_part[:DH]
            adjoint = adjoint - (folded(high[DH:]) + low_part[DH:]) + source_ref[rows, lanes]
            grad_error = -rate * slope
            gv_ref[rows, lanes] = (-grad_error).astype(BF16)
            d_hi, d_lo = split(grad_error)
            grad = part_ref[rows, lanes]
            grad += folded(times(both(d_hi, d_lo), diagonal(wt_ref[hi_rows, lanes], masks)))
            grad += times(d_hi, diagonal(wt_ref[lo_rows, lanes], masks))
            on_g = folded(times_t(e_ref[two, lanes], g_block)) + times_t(e_ref[hi_rows, lanes], g_low_block)
            gk_ref[rows, lanes] = (grad - rate * on_g).astype(BF16)
        for p in range(PAIRS):
            first = pl.multiple_of((index * PAIRS + p) * DH, DH)
            flat_ref[pl.ds(first, DH), :] = adjoint[:, p * 128 : p * 128 + 128]
            even = flat_ref[pl.ds(first, half, stride=2), :]
            odd = flat_ref[pl.ds(first + 1, half, stride=2), :]
            flat_ref[pl.ds(first, half), :] = jnp.where(low, even, pltpu.roll(odd, DH, 1))
            flat_ref[pl.ds(first + half, half), :] = jnp.where(low, pltpu.roll(even, DH, 1), odd)
        if (t + 1) * HEADS == 8:
            head = pl.multiple_of((index + 1) * HEADS - 8, 8)
            for i in range(half):
                start_ref[pl.ds(head, 8), i * 128 : (i + 1) * 128] = flat_ref[pl.ds(head * half + i, 8, stride=half), :]

    features = k_ref.shape[1]
    fetch = mover(inputs, refs[10:15], in_sems, features)
    ship = mover((gk_ref, gv_ref, start_ref), outputs, out_sems, features)
    run(work, features // QUAD, fetch, ship, pltpu.make_async_copy(rate_hbm, rate_ref, rate_sem))


def call(kernel, ins, outs, flops, scratch=(), limit=58):
    args = [array for array, _ in ins]
    size = sum(a.size * a.dtype.itemsize for a in args) + sum(o.size * o.dtype.itemsize for o, _ in outs)
    return pl.pallas_call(
        kernel,
        out_shape=tuple(shape if memory is pltpu.VMEM else pltpu.HBM(shape.shape, shape.dtype) for shape, memory in outs),
        in_specs=[pl.BlockSpec(memory_space=memory) for _, memory in ins],
        out_specs=tuple(pl.BlockSpec(memory_space=memory) for _, memory in outs),
        scratch_shapes=list(scratch),
        compiler_params=pltpu.CompilerParams(vmem_limit_bytes=limit * 1024 * 1024),
        cost_estimate=pl.CostEstimate(flops=flops, bytes_accessed=size, transcendentals=0),
    )(*args)


def per_device(queries, memory_keys, memory_values, upstream, inner_rate, checkpoints):
    sections = lax.axis_size("section")
    shards = lax.axis_size("seq")
    heads = inner_rate.shape[1]
    features = queries.shape[2]
    tokens = queries.shape[1]
    q, k, v, w = queries[0], memory_keys[0], memory_values[0], checkpoints[0, 0]

    def array(rows, kind, columns=features):
        return jax.ShapeDtypeStruct((rows, columns), kind)

    def apart(a):
        return jax.ShapeDtypeStruct((a.shape[0] * CHUNKS, a.shape[1] // CHUNKS), a.dtype)

    def buffers(arrays):
        return [pltpu.VMEM(a.shape, a.dtype) for a in arrays]

    def semaphores(count):
        return pltpu.SemaphoreType.DMA((count, CHUNKS))

    def outside(arrays):
        return [(a if isinstance(a, jax.ShapeDtypeStruct) else pltpu.with_memory_space_constraint(a, pltpu.HBM), pltpu.HBM) for a in arrays]

    def inside(arrays):
        return [(a, pltpu.VMEM) for a in arrays]

    unit = 2 * tokens * features * QUAD
    flat = pltpu.VMEM((heads * DH // 2, 128), F32)
    single, whole, double = array(tokens, F32), array(tokens, BF16), array(2 * tokens, BF16)
    rate = [pltpu.SMEM(inner_rate.shape, F32), pltpu.SemaphoreType.DMA]

    cotangent = lax.ppermute(upstream, "section", [((i + 1) % sections, i) for i in range(sections)])
    dz = cotangent[0]
    acode, ascale, mt = call(
        map_kernel,
        outside([inner_rate, q, k]),
        inside([array(DH, BF16), array(8, F32), double]),
        8 * unit,
        rate + buffers([q, k]) + [semaphores(2)],
        MAP_LIMIT,
    )
    sent, back = jax.ShapeDtypeStruct((heads, DH + 8, 128), BF16), jax.ShapeDtypeStruct((shards, DH // 2 + 8, 128), BF16)
    (packed,) = call(
        pack_kernel,
        inside([mt, dz, acode, ascale]),
        outside([sent]),
        2 * unit,
        buffers([sent]) + [pltpu.SemaphoreType.DMA((CHUNKS,))],
        24,
    )
    arrived = lax.all_to_all(packed, "seq", 0, 0, tiled=True)
    rate_later, _ = lax.optimization_barrier((inner_rate, packed))
    given, made = [q, k, v, w, dz], [double, double, single, single]
    error, weights, gate, slope, source = call(
        trail_kernel,
        outside([rate_later] + given),
        inside([double]) + outside([apart(a) for a in made]),
        10 * unit,
        rate + buffers(given + made) + [flat, semaphores(5), semaphores(4)],
        LATE_LIMIT,
    )
    arrived, slope = lax.optimization_barrier((arrived, slope))
    (ends,) = call(
        partial(relay_kernel, group=4),
        inside([arrived]),
        outside([back]),
        unit,
        buffers([back]) + [pltpu.VMEM((shards, DH, 128), F32), pltpu.VMEM((shards, DH, 256), BF16), pltpu.SemaphoreType.DMA((CHUNKS,))],
        24,
    )
    returned = lax.all_to_all(ends, "seq", 0, 0, tiled=True)
    rate_later, _ = lax.optimization_barrier((inner_rate, ends))
    grad_q, part, turned = call(
        direct_kernel,
        outside([rate_later]) + inside([error]) + outside([q, k, dz, weights]),
        outside([whole, apart(single)]) + inside([double]),
        10 * unit,
        rate + buffers([whole, whole, whole, double, whole, single]) + [semaphores(4), semaphores(2)],
        LATE_LIMIT,
    )
    held, made = [whole, double, single, single, single], [whole, whole, array(heads, F32, DH * DH)]
    grad_k, grad_v, start = call(
        final_kernel,
        outside([inner_rate]) + inside([returned, error, turned]) + outside([k, gate, slope, source, part]),
        outside(made),
        10 * unit,
        rate + buffers(held + made) + [flat, semaphores(5), semaphores(3)],
        LATE_LIMIT,
    )
    return grad_q[None], grad_k[None], grad_v[None], start[None, None]


def solution(mesh):
    tokens = P("section", "seq", None)
    return jax.shard_map(
        per_device,
        mesh=mesh,
        in_specs=(tokens, tokens, tokens, tokens, P("section", None), P("section", "seq", None, None)),
        out_specs=(tokens, tokens, tokens, P("section", "seq", None, None)),
        check_vma=False,
    )
```
